32 devices in a mesh: dp: 2 (over core), row: 4 (over y, x), col: 4 (over z).
Axes of the slice: x: 2, y: 2, z: 4, core: 2. Of those that a mesh axis runs over, the one named last changes fastest.
Arguments:
- features: bfloat16 [64, 48, 2048], P(('dp', 'row'), 'col'), parts along dimension 0, may hold values from 0 to 40
- low_level: bfloat16 [128, 96, 256], P(('dp', 'row'), 'col'), parts along dimension 0, may hold values from -6 to 6
- point_weight: bfloat16 [2048, 256], P(None, 'row'), may hold values from -0.125 to 0.125
- atrous_weight: bfloat16 [3, 3, 3, 2048, 256], P(None, None, None, None, 'row'), may hold values from -0.046875 to 0.046875
- pool_weight: bfloat16 [2048, 256], P(None, 'row'), may hold values from -0.125 to 0.125
- aspp_bias: float32 [5, 256], P(None, 'row'), may hold values from -1.5 to 1.5
- proj_weight: bfloat16 [1280, 256], replicated, may hold values from -0.15625 to 0.15625
- proj_bias: float32 [256], replicated, may hold values from -1.5 to 1.5
- low_weight: bfloat16 [256, 48], replicated, may hold values from -0.375 to 0.375
- low_bias: float32 [48], replicated, may hold values from -1.5 to 1.5
- conv1_weight: bfloat16 [3, 3, 304, 256], replicated, may hold values from -0.109375 to 0.109375
- conv1_bias: float32 [256], replicated, may hold values from -1.5 to 1.5
- conv2_weight: bfloat16 [3, 3, 256, 256], replicated, may hold values from -0.125 to 0.125
- conv2_bias: float32 [256], replicated, may hold values from -1.5 to 1.5
Outputs:
- decoded: bfloat16 [128, 96, 256], P(('dp', 'row'), 'col'), parts along dimension 0
The draws below stay inside these ranges and needn't reach their ends.
There are 2 independent parts, one for each index of `dp`. The reference program is written for one: setup_inputs(seed, part) draws one part's arguments, and reference() takes and returns one part's arrays. A program takes and returns all parts, laid end to end along the dimension named above; an argument that names none is the same for every part. Nothing has to cross between parts.
All inputs are finite; a program needn't handle non-finite values.
Results may differ from the reference program's by a relative error of at most 0.0057.
Values may be sent and summed in bfloat16 or wider, within the bound.
A program may use at most 128 MiB of HBM per device.

```python
import jax
import jax.numpy as jnp

C_IN = 2048
C_ASPP = 256
C_LOW = 256
C_RED = 48
C_DEC = 256
TR = 8
TC = 12
MAP_H = 32
MAP_W = 48


def smooth_profile(coeff_key, length):
    coefficients = jax.random.uniform(coeff_key, (2, C_IN), jnp.float32, -1.0, 1.0)
    position = 2.0 * jnp.arange(length, dtype=jnp.float32) / max(length - 1, 1) - 1.0
    linear_part = 0.5 * coefficients[0][None, :] * position[:, None]
    curved_part = 0.3 * coefficients[1][None, :] * (position[:, None] * position[:, None] - 1.0 / 3.0)
    return 1.0 + linear_part + curved_part


def draw_features(key, part):
    base_key, chan_key, level_key, row_key, col_key = jax.random.split(jax.random.fold_in(key, 11), 5)
    shape = (MAP_H, MAP_W, C_IN)
    channel_scale = jnp.exp(jax.random.uniform(chan_key, (C_IN,), jnp.float32, jnp.log(0.3), jnp.log(3.0)))
    row_trend = 1.0 + 2.0 * jnp.arange(MAP_H, dtype=jnp.float32) / max(MAP_H - 1, 1)
    tile_levels = jnp.exp(jax.random.uniform(level_key, (MAP_H // TR, MAP_W // TC), jnp.float32, jnp.log(0.6), jnp.log(1.4)))
    level_map = jnp.repeat(jnp.repeat(tile_levels, TR, axis=0), TC, axis=1)
    row_profile = smooth_profile(row_key, MAP_H)
    col_profile = smooth_profile(col_key, MAP_W)
    base_values = jnp.minimum(jnp.abs(jax.random.normal(base_key, shape, jnp.float32)) / 3.0, 1.0)
    values = base_values * channel_scale[None, None, :] * row_trend[:, None, None]
    values = values * level_map[:, :, None] * row_profile[:, None, :] * col_profile[None, :, :]
    return values.astype(jnp.bfloat16)


def shard_levels(key, shape, shards, low, largest):
    def one(dim, parts):
        draws = jax.random.uniform(jax.random.fold_in(jax.random.fold_in(key, 6), dim), (parts,), jnp.float32, low / len(shards), largest / len(shards))
        return jnp.repeat(jnp.exp(draws), shape[dim] // parts).reshape((-1,) + (1,) * (len(shape) - dim - 1))

    factor_of = one(*shards[0])
    for cut in shards[1:]:
        factor_of = factor_of * one(*cut)
    return factor_of


def scatter_about(stream_key, shape, scale, reach, shards=(), held_as=jnp.bfloat16):
    values = scale * jax.random.normal(stream_key, shape, jnp.float32)
    if shards:
        values = values * shard_levels(stream_key, shape, shards, -0.22, 0.18)
    return jnp.clip(values, -reach, reach).astype(held_as)


def setup_inputs(seed: int = 0, part: int = 0) -> dict:
    streams_of = jax.random.split(jax.random.key(seed), 15)
    part_keys = jax.random.split(jax.random.fold_in(streams_of[14], part), 15)
    features = draw_features(jax.random.fold_in(jax.random.fold_in(streams_of[14], part), 71), part)
    low_level = scatter_about(part_keys[1], (2 * MAP_H, 2 * MAP_W, C_LOW), 1.0, 6.0, ((0, 4), (1, 4)))
    point_weight = scatter_about(streams_of[2], (C_IN, C_ASPP), C_IN ** -0.5, 0.125, ((1, 4),))
    atrous_weight = scatter_about(streams_of[3], (3, 3, 3, C_IN, C_ASPP), (9 * C_IN) ** -0.5, 0.046875, ((4, 4),))
    pool_weight = scatter_about(streams_of[4], (C_IN, C_ASPP), C_IN ** -0.5, 0.125, ((1, 4),))
    aspp_bias = scatter_about(streams_of[5], (5, C_ASPP), 0.3, 1.5, ((1, 4),), jnp.float32)
    proj_weight = scatter_about(streams_of[6], (5 * C_ASPP, C_ASPP), (5 * C_ASPP) ** -0.5, 0.15625)
    proj_bias = scatter_about(streams_of[7], (C_ASPP,), 0.3, 1.5, (), jnp.float32)
    low_weight = scatter_about(streams_of[8], (C_LOW, C_RED), C_LOW ** -0.5, 0.375)
    low_bias = scatter_about(streams_of[9], (C_RED,), 0.3, 1.5, (), jnp.float32)
    conv1_weight = scatter_about(streams_of[10], (3, 3, C_ASPP + C_RED, C_DEC), (9 * (C_ASPP + C_RED)) ** -0.5, 0.109375)
    conv1_bias = scatter_about(streams_of[11], (C_DEC,), 0.3, 1.5, (), jnp.float32)
    conv2_weight = scatter_about(streams_of[12], (3, 3, C_DEC, C_DEC), (9 * C_DEC) ** -0.5, 0.125)
    conv2_bias = scatter_about(streams_of[13], (C_DEC,), 0.3, 1.5, (), jnp.float32)
    return dict(features=features, low_level=low_level, point_weight=point_weight, atrous_weight=atrous_weight, pool_weight=pool_weight, aspp_bias=aspp_bias, proj_weight=proj_weight, proj_bias=proj_bias, low_weight=low_weight, low_bias=low_bias, conv1_weight=conv1_weight, conv1_bias=conv1_bias, conv2_weight=conv2_weight, conv2_bias=conv2_bias)


RATES = (12, 24, 36)


def shifted(field, row_off, col_off):
    height, width = field.shape[0], field.shape[1]
    extent = max(abs(row_off), abs(col_off))
    padded = jnp.pad(field, ((extent, extent), (extent, extent), (0, 0)))
    return padded[extent + row_off:extent + row_off + height, extent + col_off:extent + col_off + width]


def enlarge(padded):
    values = padded.astype(jnp.float32)
    middle = values[1:-1]
    even = 0.75 * middle + 0.25 * values[:-2]
    odd = 0.75 * middle + 0.25 * values[2:]
    values = jnp.stack([even, odd], axis=1).reshape(2 * middle.shape[0], middle.shape[1], middle.shape[2])
    middle = values[:, 1:-1]
    even = 0.75 * middle + 0.25 * values[:, :-2]
    odd = 0.75 * middle + 0.25 * values[:, 2:]
    values = jnp.stack([even, odd], axis=2).reshape(values.shape[0], 2 * middle.shape[1], middle.shape[2])
    return values.astype(jnp.bfloat16)


def convolve(padded, weight, bias):
    height, width = padded.shape[0] - 2, padded.shape[1] - 2
    windows = []
    for row_tap in range(3):
        for col_tap in range(3):
            windows.append(padded[row_tap:row_tap + height, col_tap:col_tap + width])
    columns = jnp.concatenate(windows, axis=2)
    depth = columns.shape[2]
    result = jnp.dot(columns.reshape(-1, depth), weight.reshape(depth, -1), preferred_element_type=jnp.float32)
    result = jnp.maximum(result + bias, 0.0).astype(jnp.bfloat16)
    return result.reshape(height, width, -1)


def reference(features, low_level, point_weight, atrous_weight, pool_weight, aspp_bias, proj_weight, proj_bias, low_weight, low_bias, conv1_weight, conv1_bias, conv2_weight, conv2_bias):
    height, width = features.shape[0], features.shape[1]
    flat_rows = features.reshape(-1, features.shape[2])

    def activate(values, number):
        return jnp.maximum(values + aspp_bias[number], 0.0).astype(jnp.bfloat16)

    outputs = [activate(jnp.dot(flat_rows, point_weight, preferred_element_type=jnp.float32).reshape(height, width, -1), 0)]
    for rate_number in range(3):
        dilation = RATES[rate_number]
        running = jnp.zeros((height, width, point_weight.shape[1]), jnp.float32)
        for row_tap in range(3):
            for col_tap in range(3):
                term = jnp.dot(flat_rows, atrous_weight[rate_number, row_tap, col_tap], preferred_element_type=jnp.float32)
                running = running + shifted(term.reshape(height, width, -1), (row_tap - 1) * dilation, (col_tap - 1) * dilation)
        outputs.append(activate(running, rate_number + 1))
    pooled = jnp.sum(jnp.dot(flat_rows, pool_weight, preferred_element_type=jnp.float32), axis=0) / (height * width)
    pool_branch = jnp.maximum(pooled + aspp_bias[4], 0.0).astype(jnp.bfloat16)
    outputs.append(jnp.broadcast_to(pool_branch, (height, width, pool_branch.shape[0])))
    joined = jnp.concatenate(outputs, axis=2)
    coarse = jnp.dot(joined.reshape(height * width, -1), proj_weight, preferred_element_type=jnp.float32)
    coarse = jnp.maximum(coarse + proj_bias, 0.0).astype(jnp.bfloat16).reshape(height, width, -1)
    upsampled = enlarge(jnp.pad(coarse, ((1, 1), (1, 1), (0, 0)), mode="edge"))
    low_rows = low_level.reshape(-1, low_level.shape[2])
    reduced = jnp.dot(low_rows, low_weight, preferred_element_type=jnp.float32)
    reduced = jnp.maximum(reduced + low_bias, 0.0).astype(jnp.bfloat16).reshape(2 * height, 2 * width, -1)
    joined_fine = jnp.concatenate([upsampled, reduced], axis=2)
    hidden = convolve(jnp.pad(joined_fine, ((1, 1), (1, 1), (0, 0))), conv1_weight, conv1_bias)
    return convolve(jnp.pad(hidden, ((1, 1), (1, 1), (0, 0))), conv2_weight, conv2_bias)
```

```python
import functools

import jax
import jax.numpy as jnp
import numpy as np
from jax import lax
from jax.experimental import pallas as pl
from jax.experimental.pallas import tpu as pltpu
from jax.sharding import PartitionSpec as P

RATES = (12, 24, 36)
MESH = pl.DeviceIdType.MESH
F32 = jnp.float32
BF16 = jnp.bfloat16


def up16(value):
    return -(-value // 16) * 16


class Plan:
    def __init__(self, rows, cols, tile_rows, tile_cols):
        self.rows, self.cols = rows, cols
        self.tr, self.tc = tile_rows, tile_cols
        self.tile = tile_rows * tile_cols
        self.height = rows * tile_rows
        self.pixels = self.height * tile_cols
        self.half = self.pixels // 2
        self.lead = up16(2 * tile_cols)
        self.span = self.tile + 2 * self.lead
        self.cstrip = up16((tile_rows + 4) * 2)
        self.fr, self.fc = 2 * tile_rows, 2 * tile_cols
        self.wr, self.wc = self.fr + 4, self.fc + 4
        self.width = 32 * (-(-self.wc // 32))
        self.window = self.wr * self.width
        self.lhalo = 2 * self.fc
        self.low = self.wr * self.fc
        self.lstrip = up16(self.wr * 2)
        self.taps = []
        for number, rate in enumerate(RATES):
            for tap in range(3):
                if abs(tap - 1) * rate < self.height:
                    self.taps.append((number, tap))

    def upsample(self):
        own = np.zeros((9, self.window, self.span), np.float32)
        side = np.zeros((9, self.window, 2 * self.cstrip), np.float32)

        def terms(fine, length, first, last):
            if (first and fine < 0) or (last and fine >= 2 * length):
                return []
            middle = fine // 2
            other = middle - 1 if fine % 2 == 0 else middle + 1
            found = []
            for place, weight in ((middle, 0.75), (other, 0.25)):
                place = max(place, 0) if first else place
                place = min(place, length - 1) if last else place
                found.append((place, weight))
            return found

        for kind in range(9):
            top, bottom = kind // 3 == 0, kind // 3 == 2
            left, right = kind % 3 == 0, kind % 3 == 2
            for a in range(self.wr):
                for b in range(self.wc):
                    at = a * self.width + b
                    for y, wy in terms(a - 2, self.tr, top, bottom):
                        for x, wx in terms(b - 2, self.tc, left, right):
                            if x < 0:
                                side[kind, at, (y + 2) * 2 + x + 2] += wy * wx
                            elif x >= self.tc:
                                side[kind, at, self.cstrip + (y + 2) * 2 + x - self.tc] += wy * wx
                            else:
                                own[kind, at, y * self.tc + x + self.lead] += wy * wx
        return own, side

    def coarse_strips(self):
        pick = np.zeros((2 * self.cstrip, self.span), np.float32)
        for y in range(-2, self.tr + 2):
            for x in range(2):
                pick[(y + 2) * 2 + x, y * self.tc + x + self.lead] = 1
                pick[self.cstrip + (y + 2) * 2 + x, y * self.tc + self.tc - 2 + x + self.lead] = 1
        return pick

    def low_strips(self):
        pick = np.zeros((2 * self.lstrip, self.low), np.float32)
        for y in range(self.wr):
            for x in range(2):
                pick[y * 2 + x, y * self.fc + x] = 1
                pick[self.lstrip + y * 2 + x, y * self.fc + self.fc - 2 + x] = 1
        return pick

    def low_window(self):
        pick = np.zeros((self.window, self.low + 2 * self.lstrip), np.float32)
        for y in range(self.wr):
            for b in range(self.wc):
                x = b - 2
                if x < 0:
                    place = self.low + y * 2 + b
                elif x >= self.fc:
                    place = self.low + self.lstrip + y * 2 + x - self.fc
                else:
                    place = y * self.fc + x
                pick[y * self.width + b, place] = 1
        return pick


def dot(a, b):
    return jnp.dot(a, b, preferred_element_type=F32)


def kernel(
    plan,
    feat_ref, low_ref, point_ref, atrous_ref, pool_ref, aspp_bias_ref, proj_ref, proj_bias_ref,
    low_weight_ref, low_bias_ref, conv1_ref, conv1_bias_ref, conv2_ref, conv2_bias_ref,
    up_own_ref, up_side_ref, cpick_ref, lpick_ref, lwindow_ref,
    out_ref,
    gathered, staged, staged_pair, weights, low_in, proj, conv1, conv2, up_own, up_side, lwindow,
    sums, zsend, zrecv, pools, branch_pool, branches, brecv, proj_blocks,
    cstrips, crecv, low_all, lsend, reduced_window, shifted, low_part, up_window, hidden,
    local_sem, feat_send, feat_recv, z_send, z_recv, pool_send, pool_recv, bp_send, bp_recv,
    b_send, b_recv, c_send, c_recv, lr_send, lr_recv, lc_send, lc_recv,
):
    rows, cols = plan.rows, plan.cols
    tile, tc, width = plan.tile, plan.tc, plan.width
    dp, row, col = lax.axis_index("dp"), lax.axis_index("row"), lax.axis_index("col")
    depth, own = point_ref.shape
    joined = own * rows

    def row_peer(step):
        return lax.rem(row + step, rows)

    def col_peer(step):
        return lax.rem(col + step, cols)

    copies = {}
    numbered = [
        ("low", low_ref, low_in),
        ("point", point_ref, staged_pair.at[0]),
        ("pool", pool_ref, staged_pair.at[1]),
        ("feat", feat_ref, gathered.at[pl.ds(pl.multiple_of(row * tile, 16), tile)]),
        ("proj", proj_ref, proj),
        ("conv1", conv1_ref, conv1),
        ("conv2", conv2_ref, conv2),
        ("lwindow", lwindow_ref, lwindow),
    ]
    kind = jnp.where(row == 0, 0, jnp.where(row == rows - 1, 2, 1)) * 3 + jnp.where(
        col == 0, 0, jnp.where(col == cols - 1, 2, 1)
    )
    numbered.append(("up_own", up_own_ref.at[kind], up_own))
    numbered.append(("up_side", up_side_ref.at[kind], up_side))
    for place, (number, tap) in enumerate(plan.taps):
        numbered.append(("tap%d" % place, atrous_ref.at[number, tap], staged.at[place]))
    for place, (name, src, dst) in enumerate(numbered):
        copies[name] = pltpu.make_async_copy(src, dst, local_sem.at[place])
        copies[name].start()

    barrier = pltpu.get_barrier_semaphore()
    for step in range(1, rows):
        pl.semaphore_signal(barrier, inc=1, device_id=(dp, row_peer(step), col), device_id_type=MESH)
    for step in range(1, cols):
        pl.semaphore_signal(barrier, inc=1, device_id=(dp, row, col_peer(step)), device_id_type=MESH)
    pl.semaphore_wait(barrier, rows + cols - 2)

    mine = pl.ds(pl.multiple_of(row * tile, 16), tile)
    feats = []
    for step in range(1, rows):
        copy = pltpu.make_async_remote_copy(
            src_ref=feat_ref, dst_ref=gathered.at[mine],
            send_sem=feat_send.at[step - 1], recv_sem=feat_recv.at[step - 1],
            device_id=(dp, row_peer(step), col), device_id_type=MESH,
        )
        copy.start()
        feats.append(copy)

    branches[pl.ds(0, plan.lead), :] = jnp.zeros((plan.lead, 4 * own), BF16)
    branches[pl.ds(plan.lead + plan.pixels, plan.lead), :] = jnp.zeros((plan.lead, 4 * own), BF16)
    distances = [rate // tc for rate in RATES]
    for number, far in enumerate(distances):
        @pl.when(col < far)
        def _():
            zrecv[number, 0] = jnp.zeros(zrecv.shape[2:], BF16)

        @pl.when(col + far >= cols)
        def _():
            zrecv[number, 1] = jnp.zeros(zrecv.shape[2:], BF16)

    low_ends = (pl.ds(0, plan.lhalo), pl.ds(plan.low - plan.lhalo, plan.lhalo))
    low_sides = (pl.ds(plan.low, plan.lstrip), pl.ds(plan.low + plan.lstrip, plan.lstrip))
    for side, edge in ((0, row == 0), (1, row == rows - 1)):
        @pl.when(edge)
        def _():
            low_all[low_ends[side], :] = jnp.zeros((plan.lhalo, low_all.shape[1]), BF16)

    for side, edge in ((0, col == 0), (1, col == cols - 1)):
        @pl.when(edge)
        def _():
            low_all[low_sides[side], :] = jnp.zeros((plan.lstrip, low_all.shape[1]), BF16)
            crecv[side] = jnp.zeros(crecv.shape[1:], BF16)

    def pair(refs, sends, recvs, along):
        made = []
        for side in range(2):
            src, dst = refs[side]
            step = -1 if side == 0 else 1
            if along == "row":
                there = row + step >= 0 if side == 0 else row + step < rows
                target = (dp, lax.rem(row + step + rows, rows), col)
            else:
                there = col + step >= 0 if side == 0 else col + step < cols
                target = (dp, row, lax.rem(col + step + cols, cols))
            made.append((there, pltpu.make_async_remote_copy(
                src_ref=src, dst_ref=dst, send_sem=sends.at[side], recv_sem=recvs.at[1 - side],
                device_id=target, device_id_type=MESH,
            ), recvs.at[side], refs[1 - side][1]))
        return made

    def start_pair(made):
        for there, copy, _, _ in made:
            @pl.when(there)
            def _():
                copy.start()

    def wait_recv_pair(made):
        for there, copy, sem, landed in made:
            @pl.when(there)
            def _():
                pltpu.make_async_copy(landed, landed, sem).wait()

    def wait_send_pair(made):
        for there, copy, _, _ in made:
            @pl.when(there)
            def _():
                copy.wait_send()

    copies["low"].wait()
    reduced = dot(low_in[...], low_weight_ref[...]) + low_bias_ref[...]
    low_all[pl.ds(plan.lhalo, plan.fr * plan.fc), :] = jnp.maximum(reduced, 0.0).astype(BF16)
    low_rows = pair(
        (
            (low_all.at[pl.ds(plan.lhalo, plan.lhalo)], low_all.at[low_ends[1]]),
            (low_all.at[pl.ds(plan.low - 2 * plan.lhalo, plan.lhalo)], low_all.at[low_ends[0]]),
        ),
        lr_send, lr_recv, "row",
    )
    start_pair(low_rows)

    piece = min(256, depth)

    def join(place):
        number, tap = plan.taps[place]
        copies["tap%d" % place].wait()

        def body(index, carry):
            at = pl.ds(pl.multiple_of(index * piece, 16), piece)
            parts = [staged[place, j, at, :] for j in (0, 2, 1)]
            if tap == 1 and number < 2:
                parts.append(staged_pair[number, at, :])
            else:
                parts.append(jnp.zeros((piece, own), BF16))
            weights[place, at, :] = jnp.concatenate(parts, axis=1)
            return carry

        lax.fori_loop(0, depth // piece, body, 0)

    copies["point"].wait()
    copies["pool"].wait()
    for place in range(len(plan.taps)):
        join(place)

    wait_recv_pair(low_rows)
    lsend[...] = dot(lpick_ref[...], low_all[pl.ds(0, plan.low), :]).astype(BF16)
    low_cols = pair(
        (
            (lsend.at[pl.ds(0, plan.lstrip)], low_all.at[low_sides[1]]),
            (lsend.at[pl.ds(plan.lstrip, plan.lstrip)], low_all.at[low_sides[0]]),
        ),
        lc_send, lc_recv, "col",
    )
    start_pair(low_cols)

    copies["proj"].wait()
    for w in range(rows):
        for branch in range(4):
            proj_blocks[w, pl.ds(branch * own, own), :] = proj[
                pl.ds(branch * joined + w * own, own), :
            ]

    wait_recv_pair(low_cols)
    copies["lwindow"].wait()
    copies["conv1"].wait()
    reduced_window[...] = dot(lwindow[...], low_all[...]).astype(BF16)
    wide = conv1.shape[3]
    fine = wide if plan is None else conv1.shape[2] - low_all.shape[1]
    hidden_px = (plan.wr - 2) * width
    out_px = plan.fr * width
    tail = jnp.zeros((8, wide), F32)
    for j in range(2):
        shifted[j, pl.ds(hidden_px, 8), :] = tail
    for j in range(3):
        total = None
        for i in range(3):
            term = dot(
                reduced_window[pl.ds(i * width, hidden_px), :],
                conv1[i, j, pl.ds(fine, low_all.shape[1]), :],
            )
            total = term if total is None else total + term
        if j == 0:
            low_part[...] = total + conv1_bias_ref[...]
        else:
            shifted[j - 1, pl.ds(0, hidden_px), :] = total
    low_part[...] += shifted[0, pl.ds(1, hidden_px), :] + shifted[1, pl.ds(2, hidden_px), :]

    copies["feat"].wait()
    for copy in feats:
        copy.wait_recv()

    half = plan.half
    sideways = [None, None, None]
    pool_copies = []
    for number in (2, 1, 0):
        rate = RATES[number]
        for place, (which, tap) in enumerate(plan.taps):
            if which == number and tap == 1:
                sums[number] = dot(gathered[...], weights[place])
        for place, (which, tap) in enumerate(plan.taps):
            if which == number and tap != 1:
                offset = (tap - 1) * rate
                begin, end = max(0, -offset), min(plan.height, plan.height - offset)
                size = (end - begin) * tc
                sums[number, pl.ds(begin * tc, size), :] += dot(
                    gathered[pl.ds((begin + offset) * tc, size), :], weights[place]
                )
        for side in range(2):
            lanes = pl.ds(side * own, own)
            zsend[number, side] = jnp.concatenate(
                [sums[number, pl.ds(0, half), lanes], sums[number, pl.ds(half, half), lanes]], axis=1
            ).astype(BF16)
        made = []
        for side, far in ((0, distances[number]), (1, -distances[number])):
            there = col + far < cols if far > 0 else col + far >= 0
            come = col - far < cols if far < 0 else col - far >= 0
            copy = pltpu.make_async_remote_copy(
                src_ref=zsend.at[number, side], dst_ref=zrecv.at[number, side],
                send_sem=z_send.at[number, side], recv_sem=z_recv.at[number, side],
                device_id=(dp, row, lax.rem(col + far + 4 * cols, cols)), device_id_type=MESH,
            )
            made.append((there, come, copy))

            @pl.when(there)
            def _():
                copy.start()
        sideways[number] = made
        if number == 1:
            part = jnp.sum(sums[number, :, pl.ds(3 * own, own)], axis=0, keepdims=True)
            pools[col] = jnp.broadcast_to(part, (8, own))
            for step in range(1, cols):
                copy = pltpu.make_async_remote_copy(
                    src_ref=pools.at[col], dst_ref=pools.at[col],
                    send_sem=pool_send.at[step - 1], recv_sem=pool_recv.at[step - 1],
                    device_id=(dp, row, col_peer(step)), device_id_type=MESH,
                )
                copy.start()
                pool_copies.append(copy)

    for copy in pool_copies:
        copy.wait_recv()
    pooled = pools[0]
    for place in range(1, cols):
        pooled = pooled + pools[place]
    pooled = pooled / (plan.height * cols * tc)
    last = jnp.maximum(pooled + aspp_bias_ref[pl.ds(4, 1), :], 0.0)
    branch_pool[row] = jnp.concatenate([last, last], axis=0).astype(BF16)
    bp_copies = []
    for step in range(1, rows):
        copy = pltpu.make_async_remote_copy(
            src_ref=branch_pool.at[row], dst_ref=branch_pool.at[row],
            send_sem=bp_send.at[step - 1], recv_sem=bp_recv.at[step - 1],
            device_id=(dp, row_peer(step), col), device_id_type=MESH,
        )
        copy.start()
        bp_copies.append(copy)

    def bias(number):
        return aspp_bias_ref[pl.ds(number, 1), :]

    halves = []
    for part in range(2):
        at = pl.ds(part * half, half)
        halves.append([jnp.maximum(sums[0, at, pl.ds(3 * own, own)] + bias(0), 0.0).astype(BF16)])
    for number in (2, 1, 0):
        for side, (there, come, copy) in enumerate(sideways[number]):
            @pl.when(come)
            def _():
                copy.wait_recv()
    for number in range(3):
        arrived = zrecv[number, 0].astype(F32) + zrecv[number, 1].astype(F32)
        for part in range(2):
            at = pl.ds(part * half, half)
            value = sums[number, at, pl.ds(2 * own, own)] + arrived[:, part * own:(part + 1) * own]
            halves[part].append(jnp.maximum(value + bias(number + 1), 0.0).astype(BF16))
    for part in range(2):
        branches[pl.ds(plan.lead + part * half, half), :] = jnp.concatenate(halves[part], axis=1)

    b_copies = []
    for step in range(1, rows):
        start = pl.multiple_of(row_peer(step) * tile, 16)
        copy = pltpu.make_async_remote_copy(
            src_ref=branches.at[pl.ds(start, plan.span)], dst_ref=brecv.at[row],
            send_sem=b_send.at[step - 1], recv_sem=b_recv.at[step - 1],
            device_id=(dp, row_peer(step), col), device_id_type=MESH,
        )
        copy.start()
        b_copies.append(copy)
    brecv[row] = branches[pl.ds(pl.multiple_of(row * tile, 16), plan.span), :]

    for copy in bp_copies:
        copy.wait_recv()
    constant = proj_bias_ref[...]
    for w in range(rows):
        constant = constant + dot(
            branch_pool[w], proj[pl.ds(4 * joined + w * own, own), :]
        )[0:1, :]
    for copy in b_copies:
        copy.wait_recv()
    coarse = constant
    for w in range(rows):
        coarse = coarse + dot(brecv[w], proj_blocks[w])
    coarse = jnp.maximum(coarse, 0.0).astype(BF16)

    cstrips[...] = dot(cpick_ref[...], coarse).astype(BF16)
    coarse_cols = pair(
        (
            (cstrips.at[pl.ds(0, plan.cstrip)], crecv.at[1]),
            (cstrips.at[pl.ds(plan.cstrip, plan.cstrip)], crecv.at[0]),
        ),
        c_send, c_recv, "col",
    )
    start_pair(coarse_cols)
    copies["up_own"].wait()
    copies["up_side"].wait()
    copies["conv2"].wait()
    up_sums = dot(up_own[...], coarse)
    wait_recv_pair(coarse_cols)
    strips = jnp.concatenate([crecv[0], crecv[1]], axis=0)
    up_window[...] = (up_sums + dot(up_side[...], strips)).astype(BF16)

    def convolve(source, weight, depth, size):
        wide_in = jnp.concatenate(
            [source[pl.ds(i * width, size), :] for i in range(3)], axis=1
        )
        first = None
        for j in range(3):
            stacked = jnp.concatenate(
                [weight[i, j, pl.ds(0, depth), :] for i in range(3)], axis=0
            )
            total = dot(wide_in, stacked)
            if j == 0:
                first = total
            else:
                shifted[j - 1, pl.ds(0, size), :] = total
        return first + shifted[0, pl.ds(1, size), :] + shifted[1, pl.ds(2, size), :]

    result = convolve(up_window, conv1, fine, hidden_px) + low_part[...]
    result = jnp.maximum(result, 0.0).reshape(plan.wr - 2, width, wide)
    a = lax.broadcasted_iota(jnp.int32, result.shape, 0)
    b = lax.broadcasted_iota(jnp.int32, result.shape, 1)
    low_a = jnp.where(row == 0, 1, 0)
    high_a = jnp.where(row == rows - 1, plan.fr + 1, plan.fr + 2)
    low_b = jnp.where(col == 0, 1, 0)
    high_b = jnp.where(col == cols - 1, plan.fc + 1, plan.fc + 2)
    inside = (a >= low_a) & (a < high_a) & (b >= low_b) & (b < high_b)
    result = jnp.where(inside, result, 0.0)
    hidden[...] = result.reshape(hidden_px, wide).astype(BF16)

    result = convolve(hidden, conv2, conv2.shape[2], out_px) + conv2_bias_ref[...]
    result = jnp.maximum(result, 0.0).reshape(plan.fr, width, wide)
    out_ref[...] = result[:, : plan.fc, :].astype(BF16)

    for copy in feats + pool_copies + bp_copies + b_copies:
        copy.wait_send()
    for made in sideways:
        for there, come, copy in made:
            @pl.when(there)
            def _():
                copy.wait_send()
    for made in (low_rows, low_cols, coarse_cols):
        wait_send_pair(made)


def on_device(
    plan,
    features, low_level, point_weight, atrous_weight, pool_weight, aspp_bias, proj_weight, proj_bias,
    low_weight, low_bias, conv1_weight, conv1_bias, conv2_weight, conv2_bias,
):
    depth, own = point_weight.shape
    out_width = proj_weight.shape[1]
    red = low_weight.shape[1]
    rows, cols = plan.rows, plan.cols
    taps = len(plan.taps)
    wide = conv1_weight.shape[3]
    up_own, up_side = plan.upsample()
    any_spec = pl.BlockSpec(memory_space=pl.ANY)
    vmem = pl.BlockSpec(memory_space=pltpu.VMEM)
    dma = pltpu.SemaphoreType.DMA
    hidden_px = (plan.wr - 2) * plan.width
    scratch = [
        pltpu.VMEM((plan.pixels, depth), BF16),
        pltpu.VMEM((taps, 3, depth, own), BF16),
        pltpu.VMEM((2, depth, own), BF16),
        pltpu.VMEM((taps, depth, 4 * own), BF16),
        pltpu.VMEM((plan.fr * plan.fc, low_level.shape[2]), BF16),
        pltpu.VMEM(proj_weight.shape, BF16),
        pltpu.VMEM(conv1_weight.shape, BF16),
        pltpu.VMEM(conv2_weight.shape, BF16),
        pltpu.VMEM(up_own.shape[1:], BF16),
        pltpu.VMEM(up_side.shape[1:], BF16),
        pltpu.VMEM((plan.window, plan.low + 2 * plan.lstrip), BF16),
        pltpu.VMEM((3, plan.pixels, 4 * own), F32),
        pltpu.VMEM((3, 2, plan.half, 2 * own), BF16),
        pltpu.VMEM((3, 2, plan.half, 2 * own), BF16),
        pltpu.VMEM((cols, 8, own), F32),
        pltpu.VMEM((rows, 16, own), BF16),
        pltpu.VMEM((plan.pixels + 2 * plan.lead, 4 * own), BF16),
        pltpu.VMEM((rows, plan.span, 4 * own), BF16),
        pltpu.VMEM((rows, 4 * own, out_width), BF16),
        pltpu.VMEM((2 * plan.cstrip, out_width), BF16),
        pltpu.VMEM((2, plan.cstrip, out_width), BF16),
        pltpu.VMEM((plan.low + 2 * plan.lstrip, red), BF16),
        pltpu.VMEM((2 * plan.lstrip, red), BF16),
        pltpu.VMEM((plan.window, red), BF16),
        pltpu.VMEM((2, hidden_px + 8, wide), F32),
        pltpu.VMEM((hidden_px, wide), F32),
        pltpu.VMEM((plan.window, out_width), BF16),
        pltpu.VMEM((hidden_px, wide), BF16),
        dma((10 + taps,)),
        dma((rows - 1,)), dma((rows - 1,)),
        dma((3, 2)), dma((3, 2)),
        dma((cols - 1,)), dma((cols - 1,)),
        dma((rows - 1,)), dma((rows - 1,)),
        dma((rows - 1,)), dma((rows - 1,)),
        dma((2,)), dma((2,)), dma((2,)), dma((2,)), dma((2,)), dma((2,)),
    ]
    return pl.pallas_call(
        functools.partial(kernel, plan),
        out_shape=jax.ShapeDtypeStruct((plan.fr, plan.fc, wide), BF16),
        in_specs=[
            any_spec, any_spec, any_spec, any_spec, any_spec, vmem, any_spec, vmem,
            vmem, vmem, any_spec, vmem, any_spec, vmem,
            any_spec, any_spec, vmem, vmem, any_spec,
        ],
        out_specs=vmem,
        scratch_shapes=scratch,
        compiler_params=pltpu.CompilerParams(
            collective_id=0, has_side_effects=True, vmem_limit_bytes=60 * 1024 * 1024
        ),
    )(
        features.reshape(plan.tile, depth),
        low_level.reshape(plan.fr * plan.fc, low_level.shape[2]),
        point_weight, atrous_weight, pool_weight, aspp_bias, proj_weight, proj_bias[None],
        low_weight, low_bias[None], conv1_weight, conv1_bias[None], conv2_weight, conv2_bias[None],
        jnp.asarray(up_own, BF16), jnp.asarray(up_side, BF16),
        jnp.asarray(plan.coarse_strips(), BF16), jnp.asarray(plan.low_strips(), BF16),
        jnp.asarray(plan.low_window(), BF16),
    )


def solution(mesh):
    placed = (
        P(("dp", "row"), "col", None),
        P(("dp", "row"), "col", None),
        P(None, "row"),
        P(None, None, None, None, "row"),
        P(None, "row"),
        P(None, "row"),
        P(),
        P(),
        P(),
        P(),
        P(),
        P(),
        P(),
        P(),
    )

    def local(features, *others):
        plan = Plan(mesh.shape["row"], mesh.shape["col"], features.shape[0], features.shape[1])
        return on_device(plan, features, *others)

    return jax.shard_map(
        local,
        mesh=mesh,
        in_specs=placed,
        out_specs=P(("dp", "row"), "col", None),
        check_vma=False,
    )
```

```python
import functools

import jax
import jax.numpy as jnp
import numpy as np
from jax import lax
from jax.experimental import pallas as pl
from jax.experimental.pallas import tpu as pltpu
from jax.sharding import PartitionSpec as P

RATES = (12, 24, 36)
MESH = pl.DeviceIdType.MESH
F32 = jnp.float32
BF16 = jnp.bfloat16


def up16(value):
    return -(-value // 16) * 16


def table(values):
    lanes = -values.shape[-1] % 128
    return np.pad(values, [(0, 0)] * (values.ndim - 1) + [(0, lanes)])


class Plan:
    def __init__(self, rows, cols, tile_rows, tile_cols):
        self.rows, self.cols = rows, cols
        self.tr, self.tc = tile_rows, tile_cols
        self.tile = tile_rows * tile_cols
        self.height = rows * tile_rows
        self.pixels = self.height * tile_cols
        self.half = self.pixels // 2
        self.lead = up16(2 * tile_cols)
        self.span = self.tile + 2 * self.lead
        self.cstrip = up16((tile_rows + 4) * 2)
        self.fr, self.fc = 2 * tile_rows, 2 * tile_cols
        self.wr, self.wc = self.fr + 4, self.fc + 4
        self.width = 32 * (-(-self.wc // 32))
        self.window = self.wr * self.width
        self.lhalo = 2 * self.fc
        self.low = self.wr * self.fc
        self.lstrip = up16(self.wr * 2)
        self.taps = []
        for number, rate in enumerate(RATES):
            for tap in range(3):
                if abs(tap - 1) * rate < self.height:
                    self.taps.append((number, tap))

    def upsample(self):
        own = np.zeros((9, self.window, self.span), np.float32)
        side = np.zeros((9, self.window, 2 * self.cstrip), np.float32)

        def terms(fine, length, first, last):
            if (first and fine < 0) or (last and fine >= 2 * length):
                return []
            middle = fine // 2
            other = middle - 1 if fine % 2 == 0 else middle + 1
            found = []
            for place, weight in ((middle, 0.75), (other, 0.25)):
                place = max(place, 0) if first else place
                place = min(place, length - 1) if last else place
                found.append((place, weight))
            return found

        for kind in range(9):
            top, bottom = kind // 3 == 0, kind // 3 == 2
            left, right = kind % 3 == 0, kind % 3 == 2
            for a in range(self.wr):
                for b in range(self.wc):
                    at = a * self.width + b
                    for y, wy in terms(a - 2, self.tr, top, bottom):
                        for x, wx in terms(b - 2, self.tc, left, right):
                            if x < 0:
                                side[kind, at, (y + 2) * 2 + x + 2] += wy * wx
                            elif x >= self.tc:
                                side[kind, at, self.cstrip + (y + 2) * 2 + x - self.tc] += wy * wx
                            else:
                                own[kind, at, self.pixel(y, x)] += wy * wx
        return table(own), table(side)

    def pixel(self, y, x):
        if y < 0:
            return x * 2 + y + 2
        if y >= self.tr:
            return self.lead + self.tile + x * 2 + y - self.tr
        return self.lead + x * self.tr + y

    def row_strips(self):
        pick = np.zeros((2 * self.lead, self.tile), np.float32)
        for x in range(self.tc):
            for y in range(2):
                pick[x * 2 + y, x * self.tr + self.tr - 2 + y] = 1
                pick[self.lead + x * 2 + y, x * self.tr + y] = 1
        return table(pick)

    def coarse_strips(self):
        pick = np.zeros((2 * self.cstrip, self.span), np.float32)
        for y in range(-2, self.tr + 2):
            for x in range(2):
                pick[(y + 2) * 2 + x, self.pixel(y, x)] = 1
                pick[self.cstrip + (y + 2) * 2 + x, self.pixel(y, self.tc - 2 + x)] = 1
        return table(pick)

    def low_strips(self):
        pick = np.zeros((2 * self.lstrip, self.low), np.float32)
        for y in range(self.wr):
            for x in range(2):
                pick[y * 2 + x, y * self.fc + x] = 1
                pick[self.lstrip + y * 2 + x, y * self.fc + self.fc - 2 + x] = 1
        return table(pick)

    def low_window(self):
        pick = np.zeros((self.window, self.low + 2 * self.lstrip), np.float32)
        for y in range(self.wr):
            for b in range(self.wc):
                x = b - 2
                if x < 0:
                    place = self.low + y * 2 + b
                elif x >= self.fc:
                    place = self.low + self.lstrip + y * 2 + x - self.fc
                else:
                    place = y * self.fc + x
                pick[y * self.width + b, place] = 1
        return table(pick)


def dot(a, b):
    return jnp.dot(a, b, preferred_element_type=F32)


def dot_t(a, b):
    return lax.dot_general(a, b, (((1,), (1,)), ((), ())), preferred_element_type=F32)


def kernel(
    plan,
    feat_ref, low_ref, point_ref, atrous_ref, pool_ref, aspp_bias_ref, proj_ref, proj_bias_ref,
    low_weight_ref, low_bias_ref, conv1_ref, conv1_bias_ref, conv2_ref, conv2_bias_ref,
    up_own_ref, up_side_ref, rpick_ref, cpick_ref, lpick_ref, lwindow_ref,
    out_ref,
    gathered, weights, low_in, proj, conv1, conv2, up_own, up_side, lwindow,
    sums, zsend, zrecv, pools, branch_pool, branches, brecv, proj_blocks,
    cstrips, crecv, low_all, lsend, reduced_window, shifted, low_part, up_window, hidden,
    local_sem, feat_send, feat_recv, z_send, z_recv, pool_send, pool_recv, bp_send, bp_recv,
    b_send, b_recv, c_send, c_recv, lr_send, lr_recv, lc_send, lc_recv,
):
    rows, cols = plan.rows, plan.cols
    tile, tc, width = plan.tile, plan.tc, plan.width
    dp, row, col = lax.axis_index("dp"), lax.axis_index("row"), lax.axis_index("col")
    own, depth = point_ref.shape
    joined = own * rows

    def row_peer(step):
        return lax.rem(row + step, rows)

    def col_peer(step):
        return lax.rem(col + step, cols)

    copies = {}
    numbered = [
        ("low", low_ref, low_in),
        ("feat", feat_ref, gathered.at[pl.ds(pl.multiple_of(row * tile, 16), tile)]),
        ("proj", proj_ref, proj),
        ("conv1", conv1_ref, conv1),
        ("conv2", conv2_ref, conv2),
        ("lwindow", lwindow_ref, lwindow),
    ]
    kind = jnp.where(row == 0, 0, jnp.where(row == rows - 1, 2, 1)) * 3 + jnp.where(
        col == 0, 0, jnp.where(col == cols - 1, 2, 1)
    )
    numbered.append(("up_own", up_own_ref.at[kind], up_own))
    numbered.append(("up_side", up_side_ref.at[kind], up_side))
    for place, (number, tap) in enumerate(plan.taps):
        for slot, j in enumerate((0, 2, 1)):
            numbered.append((
                ("tap", place, slot), atrous_ref.at[number, tap, j],
                weights.at[place, pl.ds(slot * own, own)],
            ))
        if tap == 1 and number < 2:
            numbered.append((
                ("tap", place, 3), (point_ref, pool_ref)[number], weights.at[place, pl.ds(3 * own, own)]
            ))
        else:
            weights[place, pl.ds(3 * own, own), :] = jnp.zeros((own, depth), BF16)
    for place, (name, src, dst) in enumerate(numbered):
        copies[name] = pltpu.make_async_copy(src, dst, local_sem.at[place])
        copies[name].start()

    barrier = pltpu.get_barrier_semaphore()
    for step in range(1, rows):
        pl.semaphore_signal(barrier, inc=1, device_id=(dp, row_peer(step), col), device_id_type=MESH)
    for step in range(1, cols):
        pl.semaphore_signal(barrier, inc=1, device_id=(dp, row, col_peer(step)), device_id_type=MESH)
    pl.semaphore_wait(barrier, rows + cols - 2)

    def block(owner, part=0, parts=1):
        size = tile // parts
        return pl.ds(pl.multiple_of(owner * tile + part * size, 16), size)

    def send_block(src, owner, part, parts, target, at):
        copy = pltpu.make_async_remote_copy(
            src_ref=src, dst_ref=gathered.at[block(owner, part, parts)],
            send_sem=feat_send.at[at], recv_sem=feat_recv.at[at],
            device_id=(dp, target, col), device_id_type=MESH,
        )
        copy.start()
        return copy

    feats = []
    passing = rows == 4
    if passing:
        beside = row + 1 - 2 * lax.rem(row, 2)
        across = row + 2 - 4 * (row // 2)
        size = tile // 2
        ends = [feat_ref.at[pl.ds(part * size, size)] for part in range(2)]
        feats.append(send_block(ends[0], row, 0, 2, beside, 0))
        feats.append(send_block(ends[1], row, 1, 2, across, 2))
        feats.append(send_block(ends[1], row, 1, 2, beside, 1))
        feats.append(send_block(ends[0], row, 0, 2, across, 3))
    else:
        for step in range(1, rows):
            feats.append(send_block(feat_ref, row, 0, 1, row_peer(step), step - 1))

    def pass_on():
        if passing:
            feats[0].wait_recv()
            feats.append(send_block(gathered.at[block(beside, 0, 2)], beside, 0, 2, across, 4))
            feats[1].wait_recv()
            feats.append(send_block(gathered.at[block(across, 1, 2)], across, 1, 2, beside, 5))

    branches[0, pl.ds(0, plan.lead), :] = jnp.zeros((plan.lead, 4 * own), BF16)
    branches[rows - 1, pl.ds(plan.lead + tile, plan.lead), :] = jnp.zeros((plan.lead, 4 * own), BF16)
    distances = [rate // tc for rate in RATES]
    for number, far in enumerate(distances):
        @pl.when(col < far)
        def _():
            zrecv[number, 0] = jnp.zeros(zrecv.shape[2:], BF16)

        @pl.when(col + far >= cols)
        def _():
            zrecv[number, 1] = jnp.zeros(zrecv.shape[2:], BF16)

    low_ends = (pl.ds(0, plan.lhalo), pl.ds(plan.low - plan.lhalo, plan.lhalo))
    low_sides = (pl.ds(plan.low, plan.lstrip), pl.ds(plan.low + plan.lstrip, plan.lstrip))
    for side, edge in ((0, row == 0), (1, row == rows - 1)):
        @pl.when(edge)
        def _():
            low_all[low_ends[side], :] = jnp.zeros((plan.lhalo, low_all.shape[1]), BF16)

    for side, edge in ((0, col == 0), (1, col == cols - 1)):
        @pl.when(edge)
        def _():
            low_all[low_sides[side], :] = jnp.zeros((plan.lstrip, low_all.shape[1]), BF16)
            crecv[side] = jnp.zeros(crecv.shape[1:], BF16)

    def pair(refs, sends, recvs, along):
        made = []
        for side in range(2):
            src, dst = refs[side]
            step = -1 if side == 0 else 1
            if along == "row":
                there = row + step >= 0 if side == 0 else row + step < rows
                target = (dp, lax.rem(row + step + rows, rows), col)
            else:
                there = col + step >= 0 if side == 0 else col + step < cols
                target = (dp, row, lax.rem(col + step + cols, cols))
            made.append((there, pltpu.make_async_remote_copy(
                src_ref=src, dst_ref=dst, send_sem=sends.at[side], recv_sem=recvs.at[1 - side],
                device_id=target, device_id_type=MESH,
            ), recvs.at[side], refs[1 - side][1]))
        return made

    def start_pair(made):
        for there, copy, _, _ in made:
            @pl.when(there)
            def _():
                copy.start()

    def wait_recv_pair(made):
        for there, copy, sem, landed in made:
            @pl.when(there)
            def _():
                pltpu.make_async_copy(landed, landed, sem).wait()

    def wait_send_pair(made):
        for there, copy, _, _ in made:
            @pl.when(there)
            def _():
                copy.wait_send()

    copies["low"].wait()
    reduced = dot_t(low_in[...], low_weight_ref[...]) + low_bias_ref[...]
    low_all[pl.ds(plan.lhalo, plan.fr * plan.fc), :] = jnp.maximum(reduced, 0.0).astype(BF16)
    low_rows = pair(
        (
            (low_all.at[pl.ds(plan.lhalo, plan.lhalo)], low_all.at[low_ends[1]]),
            (low_all.at[pl.ds(plan.low - 2 * plan.lhalo, plan.lhalo)], low_all.at[low_ends[0]]),
        ),
        lr_send, lr_recv, "row",
    )
    start_pair(low_rows)

    pass_on()
    wait_recv_pair(low_rows)
    lsend[...] = dot(lpick_ref[:, pl.ds(0, plan.low)], low_all[pl.ds(0, plan.low), :]).astype(BF16)
    low_cols = pair(
        (
            (lsend.at[pl.ds(0, plan.lstrip)], low_all.at[low_sides[1]]),
            (lsend.at[pl.ds(plan.lstrip, plan.lstrip)], low_all.at[low_sides[0]]),
        ),
        lc_send, lc_recv, "col",
    )
    start_pair(low_cols)

    copies["proj"].wait()
    for w in range(rows):
        for branch in range(4):
            proj_blocks[w, pl.ds(branch * own, own), :] = proj[
                pl.ds(branch * joined + w * own, own), :
            ]

    wait_recv_pair(low_cols)
    copies["lwindow"].wait()
    copies["conv1"].wait()
    reduced_window[...] = dot(lwindow[:, pl.ds(0, low_all.shape[0])], low_all[...]).astype(BF16)
    wide = conv1.shape[3]
    fine = conv1.shape[2] - low_all.shape[1]
    hidden_px = (plan.wr - 2) * width
    out_px = plan.fr * width
    tail = jnp.zeros((8, wide), F32)
    for j in range(2):
        shifted[j, pl.ds(hidden_px, 8), :] = tail
    for j in range(3):
        total = None
        for i in range(3):
            term = dot(
                reduced_window[pl.ds(i * width, hidden_px), :],
                conv1[i, j, pl.ds(fine, low_all.shape[1]), :],
            )
            total = term if total is None else total + term
        if j == 0:
            low_part[...] = total + conv1_bias_ref[...]
        else:
            shifted[j - 1, pl.ds(0, hidden_px), :] = total
    low_part[...] += shifted[0, pl.ds(1, hidden_px), :] + shifted[1, pl.ds(2, hidden_px), :]

    copies["feat"].wait()
    for name, copy in copies.items():
        if name[0] == "tap":
            copy.wait()
    for copy in feats[2 if passing else 0:]:
        copy.wait_recv()

    half = plan.half
    sideways = [None, None, None]
    pool_copies = []
    for number in (2, 1, 0):
        rate = RATES[number]
        for place, (which, tap) in enumerate(plan.taps):
            if which == number and tap == 1:
                sums[number] = dot_t(gathered[...], weights[place])
        for place, (which, tap) in enumerate(plan.taps):
            if which == number and tap != 1:
                offset = (tap - 1) * rate
                whole, rest = offset // plan.tr, offset % plan.tr
                used = [whole, whole + 1] if rest else [whole]
                first = max(0, used[0])
                final = min(rows, rows + used[-1])
                size = (final - first) * tile
                term = dot_t(gathered[pl.ds(first * tile, size), :], weights[place])
                if rest:
                    term = term.reshape(size // plan.tr, plan.tr, 4 * own)
                    term = pltpu.roll(term, plan.tr - rest, 1)
                    upper = lax.broadcasted_iota(jnp.int32, term.shape, 1) < plan.tr - rest
                    terms = [jnp.where(upper, term, 0.0), jnp.where(upper, 0.0, term)]
                    terms = [value.reshape(size, 4 * own) for value in terms]
                else:
                    terms = [term]
                for step, value in zip(used, terms):
                    begin, end = max(0, -step), min(rows, rows - step)
                    count = (end - begin) * tile
                    if count > 0:
                        skip = (begin + step - first) * tile
                        sums[number, pl.ds(begin * tile, count), :] += value[skip:skip + count]
        for side in range(2):
            lanes = pl.ds(side * own, own)
            zsend[number, side] = jnp.concatenate(
                [sums[number, pl.ds(0, half), lanes], sums[number, pl.ds(half, half), lanes]], axis=1
            ).astype(BF16)
        made = []
        for side, far in ((0, distances[number]), (1, -distances[number])):
            there = col + far < cols if far > 0 else col + far >= 0
            come = col - far < cols if far < 0 else col - far >= 0
            copy = pltpu.make_async_remote_copy(
                src_ref=zsend.at[number, side], dst_ref=zrecv.at[number, side],
                send_sem=z_send.at[number, side], recv_sem=z_recv.at[number, side],
                device_id=(dp, row, lax.rem(col + far + 4 * cols, cols)), device_id_type=MESH,
            )
            made.append((there, come, copy))

            @pl.when(there)
            def _():
                copy.start()
        sideways[number] = made
        if number == 1:
            part = jnp.sum(sums[number, :, pl.ds(3 * own, own)], axis=0, keepdims=True)
            pools[col] = jnp.broadcast_to(part, (8, own))
            for step in range(1, cols):
                copy = pltpu.make_async_remote_copy(
                    src_ref=pools.at[col], dst_ref=pools.at[col],
                    send_sem=pool_send.at[step - 1], recv_sem=pool_recv.at[step - 1],
                    device_id=(dp, row, col_peer(step)), device_id_type=MESH,
                )
                copy.start()
                pool_copies.append(copy)

    for copy in pool_copies:
        copy.wait_recv()
    pooled = pools[0]
    for place in range(1, cols):
        pooled = pooled + pools[place]
    pooled = pooled / (plan.height * cols * tc)
    last = jnp.maximum(pooled + aspp_bias_ref[pl.ds(4, 1), :], 0.0)
    branch_pool[row] = jnp.concatenate([last, last], axis=0).astype(BF16)
    bp_copies = []
    for step in range(1, rows):
        copy = pltpu.make_async_remote_copy(
            src_ref=branch_pool.at[row], dst_ref=branch_pool.at[row],
            send_sem=bp_send.at[step - 1], recv_sem=bp_recv.at[step - 1],
            device_id=(dp, row_peer(step), col), device_id_type=MESH,
        )
        copy.start()
        bp_copies.append(copy)

    def bias(number):
        return aspp_bias_ref[pl.ds(number, 1), :]

    halves = []
    for part in range(2):
        at = pl.ds(part * half, half)
        halves.append([jnp.maximum(sums[0, at, pl.ds(3 * own, own)] + bias(0), 0.0).astype(BF16)])
    for number in (2, 1, 0):
        for side, (there, come, copy) in enumerate(sideways[number]):
            @pl.when(come)
            def _():
                copy.wait_recv()
    for number in range(3):
        arrived = zrecv[number, 0].astype(F32) + zrecv[number, 1].astype(F32)
        for part in range(2):
            at = pl.ds(part * half, half)
            value = sums[number, at, pl.ds(2 * own, own)] + arrived[:, part * own:(part + 1) * own]
            halves[part].append(jnp.maximum(value + bias(number + 1), 0.0).astype(BF16))
    joint = [jnp.concatenate(halves[part], axis=1) for part in range(2)]
    joint = jnp.concatenate(joint, axis=0)
    for place in range(rows):
        value = joint[place * tile:(place + 1) * tile]
        branches[place, pl.ds(plan.lead, tile), :] = value
        ends = dot(rpick_ref[:, pl.ds(0, tile)], value).astype(BF16)
        if place + 1 < rows:
            branches[place + 1, pl.ds(0, plan.lead), :] = ends[: plan.lead]
        if place > 0:
            branches[place - 1, pl.ds(plan.lead + tile, plan.lead), :] = ends[plan.lead:]

    b_copies = []
    for step in range(1, rows):
        copy = pltpu.make_async_remote_copy(
            src_ref=branches.at[row_peer(step)], dst_ref=brecv.at[row],
            send_sem=b_send.at[step - 1], recv_sem=b_recv.at[step - 1],
            device_id=(dp, row_peer(step), col), device_id_type=MESH,
        )
        copy.start()
        b_copies.append(copy)
    brecv[row] = branches[row]

    for copy in bp_copies:
        copy.wait_recv()
    constant = proj_bias_ref[...]
    for w in range(rows):
        constant = constant + dot(
            branch_pool[w], proj[pl.ds(4 * joined + w * own, own), :]
        )[0:1, :]
    for copy in b_copies:
        copy.wait_recv()
    coarse = constant
    for w in range(rows):
        coarse = coarse + dot(brecv[w], proj_blocks[w])
    coarse = jnp.maximum(coarse, 0.0).astype(BF16)

    cstrips[...] = dot(cpick_ref[:, pl.ds(0, plan.span)], coarse).astype(BF16)
    coarse_cols = pair(
        (
            (cstrips.at[pl.ds(0, plan.cstrip)], crecv.at[1]),
            (cstrips.at[pl.ds(plan.cstrip, plan.cstrip)], crecv.at[0]),
        ),
        c_send, c_recv, "col",
    )
    start_pair(coarse_cols)
    copies["up_own"].wait()
    copies["up_side"].wait()
    copies["conv2"].wait()
    up_sums = dot(up_own[:, pl.ds(0, plan.span)], coarse)
    wait_recv_pair(coarse_cols)
    strips = jnp.concatenate([crecv[0], crecv[1]], axis=0)
    up_window[...] = (up_sums + dot(up_side[:, pl.ds(0, 2 * plan.cstrip)], strips)).astype(BF16)

    def convolve(source, weight, depth, size):
        wide_in = jnp.concatenate(
            [source[pl.ds(i * width, size), :] for i in range(3)], axis=1
        )
        first = None
        for j in range(3):
            stacked = jnp.concatenate(
                [weight[i, j, pl.ds(0, depth), :] for i in range(3)], axis=0
            )
            total = dot(wide_in, stacked)
            if j == 0:
                first = total
            else:
                shifted[j - 1, pl.ds(0, size), :] = total
        return first + shifted[0, pl.ds(1, size), :] + shifted[1, pl.ds(2, size), :]

    result = convolve(up_window, conv1, fine, hidden_px) + low_part[...]
    result = jnp.maximum(result, 0.0).reshape(plan.wr - 2, width, wide)
    a = lax.broadcasted_iota(jnp.int32, result.shape, 0)
    b = lax.broadcasted_iota(jnp.int32, result.shape, 1)
    low_a = jnp.where(row == 0, 1, 0)
    high_a = jnp.where(row == rows - 1, plan.fr + 1, plan.fr + 2)
    low_b = jnp.where(col == 0, 1, 0)
    high_b = jnp.where(col == cols - 1, plan.fc + 1, plan.fc + 2)
    inside = (a >= low_a) & (a < high_a) & (b >= low_b) & (b < high_b)
    result = jnp.where(inside, result, 0.0)
    hidden[...] = result.reshape(hidden_px, wide).astype(BF16)

    result = convolve(hidden, conv2, conv2.shape[2], out_px) + conv2_bias_ref[...]
    result = jnp.maximum(result, 0.0).reshape(plan.fr, width, wide)
    out_ref[...] = result[:, : plan.fc, :].astype(BF16)

    for copy in feats + pool_copies + bp_copies + b_copies:
        copy.wait_send()
    for made in sideways:
        for there, come, copy in made:
            @pl.when(there)
            def _():
                copy.wait_send()
    for made in (low_rows, low_cols, coarse_cols):
        wait_send_pair(made)


def on_device(
    plan,
    features, low_level, point_weight, atrous_weight, pool_weight, aspp_bias, proj_weight, proj_bias,
    low_weight, low_bias, conv1_weight, conv1_bias, conv2_weight, conv2_bias,
):
    own, depth = point_weight.shape[::-1]
    out_width = proj_weight.shape[1]
    red = low_weight.shape[1]
    rows, cols = plan.rows, plan.cols
    taps = len(plan.taps)
    wide = conv1_weight.shape[3]
    up_own, up_side = plan.upsample()
    any_spec = pl.BlockSpec(memory_space=pl.ANY)
    vmem = pl.BlockSpec(memory_space=pltpu.VMEM)
    dma = pltpu.SemaphoreType.DMA
    hidden_px = (plan.wr - 2) * plan.width
    feat_sends = 6 if rows == 4 else rows - 1
    scratch = [
        pltpu.VMEM((plan.pixels, depth), BF16),
        pltpu.VMEM((taps, 4 * own, depth), BF16),
        pltpu.VMEM((plan.fr * plan.fc, low_level.shape[2]), BF16),
        pltpu.VMEM(proj_weight.shape, BF16),
        pltpu.VMEM(conv1_weight.shape, BF16),
        pltpu.VMEM(conv2_weight.shape, BF16),
        pltpu.VMEM(up_own.shape[1:], BF16),
        pltpu.VMEM(up_side.shape[1:], BF16),
        pltpu.VMEM(plan.low_window().shape, BF16),
        pltpu.VMEM((3, plan.pixels, 4 * own), F32),
        pltpu.VMEM((3, 2, plan.half, 2 * own), BF16),
        pltpu.VMEM((3, 2, plan.half, 2 * own), BF16),
        pltpu.VMEM((cols, 8, own), F32),
        pltpu.VMEM((rows, 16, own), BF16),
        pltpu.VMEM((rows, plan.span, 4 * own), BF16),
        pltpu.VMEM((rows, plan.span, 4 * own), BF16),
        pltpu.VMEM((rows, 4 * own, out_width), BF16),
        pltpu.VMEM((2 * plan.cstrip, out_width), BF16),
        pltpu.VMEM((2, plan.cstrip, out_width), BF16),
        pltpu.VMEM((plan.low + 2 * plan.lstrip, red), BF16),
        pltpu.VMEM((2 * plan.lstrip, red), BF16),
        pltpu.VMEM((plan.window, red), BF16),
        pltpu.VMEM((2, hidden_px + 8, wide), F32),
        pltpu.VMEM((hidden_px, wide), F32),
        pltpu.VMEM((plan.window, out_width), BF16),
        pltpu.VMEM((hidden_px, wide), BF16),
        dma((8 + 4 * taps,)),
        dma((feat_sends,)), dma((feat_sends,)),
        dma((3, 2)), dma((3, 2)),
        dma((cols - 1,)), dma((cols - 1,)),
        dma((rows - 1,)), dma((rows - 1,)),
        dma((rows - 1,)), dma((rows - 1,)),
        dma((2,)), dma((2,)), dma((2,)), dma((2,)), dma((2,)), dma((2,)),
    ]
    return pl.pallas_call(
        functools.partial(kernel, plan),
        out_shape=jax.ShapeDtypeStruct((plan.fr, plan.fc, wide), BF16),
        in_specs=[
            any_spec, any_spec, any_spec, any_spec, any_spec, vmem, any_spec, vmem,
            vmem, vmem, any_spec, vmem, any_spec, vmem,
            any_spec, any_spec, vmem, vmem, vmem, any_spec,
        ],
        out_specs=vmem,
        scratch_shapes=scratch,
        compiler_params=pltpu.CompilerParams(
            collective_id=0, has_side_effects=True, vmem_limit_bytes=60 * 1024 * 1024
        ),
    )(
        jnp.transpose(features, (1, 0, 2)).reshape(plan.tile, depth),
        low_level.reshape(plan.fr * plan.fc, low_level.shape[2]),
        point_weight.T, jnp.swapaxes(atrous_weight, 3, 4), pool_weight.T, aspp_bias, proj_weight,
        proj_bias[None], low_weight.T, low_bias[None], conv1_weight, conv1_bias[None], conv2_weight, conv2_bias[None],
        jnp.asarray(up_own, BF16), jnp.asarray(up_side, BF16),
        jnp.asarray(plan.row_strips(), BF16), jnp.asarray(plan.coarse_strips(), BF16), jnp.asarray(plan.low_strips(), BF16),
        jnp.asarray(plan.low_window(), BF16),
    )


def solution(mesh):
    placed = (
        P(("dp", "row"), "col", None),
        P(("dp", "row"), "col", None),
        P(None, "row"),
        P(None, None, None, None, "row"),
        P(None, "row"),
        P(None, "row"),
        P(),
        P(),
        P(),
        P(),
        P(),
        P(),
        P(),
        P(),
    )

    def local(features, *others):
        plan = Plan(mesh.shape["row"], mesh.shape["col"], features.shape[0], features.shape[1])
        return on_device(plan, features, *others)

    return jax.shard_map(
        local,
        mesh=mesh,
        in_specs=placed,
        out_specs=P(("dp", "row"), "col", None),
        check_vma=False,
    )
```

```python
import functools

import jax
import jax.numpy as jnp
import numpy as np
from jax import lax
from jax.experimental import pallas as pl
from jax.experimental.pallas import tpu as pltpu
from jax.sharding import PartitionSpec as P

RATES = (12, 24, 36)
MESH = pl.DeviceIdType.MESH
F32 = jnp.float32
BF16 = jnp.bfloat16


def up16(value):
    return -(-value // 16) * 16


def table(values):
    lanes = -values.shape[-1] % 128
    return np.pad(values, [(0, 0)] * (values.ndim - 1) + [(0, lanes)])


class Plan:
    def __init__(self, rows, cols, tile_rows, tile_cols):
        self.rows, self.cols = rows, cols
        self.tr, self.tc = tile_rows, tile_cols
        self.tile = tile_rows * tile_cols
        self.height = rows * tile_rows
        self.pixels = self.height * tile_cols
        self.half = self.pixels // 2
        self.lead = up16(2 * tile_cols)
        self.span = self.tile + 2 * self.lead
        self.cstrip = up16((tile_rows + 4) * 2)
        self.fr, self.fc = 2 * tile_rows, 2 * tile_cols
        self.wr, self.wc = self.fr + 4, self.fc + 4
        self.width = 32 * (-(-self.wc // 32))
        self.window = self.wr * self.width
        self.lhalo = 2 * self.fc
        self.low = self.wr * self.fc
        self.lstrip = up16(self.wr * 2)
        self.taps = []
        for number, rate in enumerate(RATES):
            for tap in range(3):
                if abs(tap - 1) * rate < self.height:
                    self.taps.append((number, tap))

    def upsample(self):
        own = np.zeros((9, self.window, self.span), np.float32)
        side = np.zeros((9, self.window, 2 * self.cstrip), np.float32)

        def terms(fine, length, first, last):
            if (first and fine < 0) or (last and fine >= 2 * length):
                return []
            middle = fine // 2
            other = middle - 1 if fine % 2 == 0 else middle + 1
            found = []
            for place, weight in ((middle, 0.75), (other, 0.25)):
                place = max(place, 0) if first else place
                place = min(place, length - 1) if last else place
                found.append((place, weight))
            return found

        for kind in range(9):
            top, bottom = kind // 3 == 0, kind // 3 == 2
            left, right = kind % 3 == 0, kind % 3 == 2
            for a in range(self.wr):
                for b in range(self.wc):
                    at = a * self.width + b
                    for y, wy in terms(a - 2, self.tr, top, bottom):
                        for x, wx in terms(b - 2, self.tc, left, right):
                            if x < 0:
                                side[kind, at, (y + 2) * 2 + x + 2] += wy * wx
                            elif x >= self.tc:
                                side[kind, at, self.cstrip + (y + 2) * 2 + x - self.tc] += wy * wx
                            else:
                                own[kind, at, self.pixel(y, x)] += wy * wx
        return table(own), table(side)

    def pixel(self, y, x):
        if y < 0:
            return x * 2 + y + 2
        if y >= self.tr:
            return self.lead + self.tile + x * 2 + y - self.tr
        return self.lead + x * self.tr + y

    def row_strips(self):
        pick = np.zeros((2 * self.lead, self.tile), np.float32)
        for x in range(self.tc):
            for y in range(2):
                pick[x * 2 + y, x * self.tr + self.tr - 2 + y] = 1
                pick[self.lead + x * 2 + y, x * self.tr + y] = 1
        return table(pick)

    def coarse_strips(self):
        pick = np.zeros((2 * self.cstrip, self.span), np.float32)
        for y in range(-2, self.tr + 2):
            for x in range(2):
                pick[(y + 2) * 2 + x, self.pixel(y, x)] = 1
                pick[self.cstrip + (y + 2) * 2 + x, self.pixel(y, self.tc - 2 + x)] = 1
        return table(pick)

    def low_strips(self):
        pick = np.zeros((2 * self.lstrip, self.low), np.float32)
        for y in range(self.wr):
            for x in range(2):
                pick[y * 2 + x, y * self.fc + x] = 1
                pick[self.lstrip + y * 2 + x, y * self.fc + self.fc - 2 + x] = 1
        return table(pick)

    def low_window(self):
        pick = np.zeros((self.window, self.low + 2 * self.lstrip), np.float32)
        for y in range(self.wr):
            for b in range(self.wc):
                x = b - 2
                if x < 0:
                    place = self.low + y * 2 + b
                elif x >= self.fc:
                    place = self.low + self.lstrip + y * 2 + x - self.fc
                else:
                    place = y * self.fc + x
                pick[y * self.width + b, place] = 1
        return table(pick)


def dot(a, b):
    return jnp.dot(a, b, preferred_element_type=F32)


def dot_t(a, b):
    return lax.dot_general(a, b, (((1,), (1,)), ((), ())), preferred_element_type=F32)


def kernel(
    plan,
    feat_ref, low_ref, point_ref, atrous_ref, pool_ref, aspp_bias_ref, proj_ref, proj_bias_ref,
    low_weight_ref, low_bias_ref, conv1_ref, conv1_bias_ref, conv2_ref, conv2_bias_ref,
    up_own_ref, up_side_ref, rpick_ref, cpick_ref, lpick_ref, lwindow_ref,
    out_ref,
    gathered, weights, low_in, proj, conv1, conv2, up_own, up_side, lwindow,
    sums, zsend, zrecv, pools, branch_pool, branches, brecv, proj_blocks,
    cstrips, crecv, low_all, lsend, reduced_window, shifted, low_part, up_window, hidden,
    local_sem, feat_send, feat_recv, z_send, z_recv, pool_send, pool_recv, bp_send, bp_recv,
    b_send, b_recv, c_send, c_recv, lr_send, lr_recv, lc_send, lc_recv,
):
    rows, cols = plan.rows, plan.cols
    tile, tc, width = plan.tile, plan.tc, plan.width
    dp, row, col = lax.axis_index("dp"), lax.axis_index("row"), lax.axis_index("col")
    own, depth = point_ref.shape
    joined = own * rows

    def row_peer(step):
        return lax.rem(row + step, rows)

    def col_peer(step):
        return lax.rem(col + step, cols)

    barrier = pltpu.get_barrier_semaphore()
    for step in range(1, rows):
        pl.semaphore_signal(barrier, inc=1, device_id=(dp, row_peer(step), col), device_id_type=MESH)
    for step in range(1, cols):
        pl.semaphore_signal(barrier, inc=1, device_id=(dp, row, col_peer(step)), device_id_type=MESH)
    pl.semaphore_wait(barrier, rows + cols - 2)

    def block(owner, part=0, parts=1):
        size = tile // parts
        return pl.ds(pl.multiple_of(owner * tile + part * size, 16), size)

    def send_block(src, owner, part, parts, target, at):
        copy = pltpu.make_async_remote_copy(
            src_ref=src, dst_ref=gathered.at[block(owner, part, parts)],
            send_sem=feat_send.at[at], recv_sem=feat_recv.at[at],
            device_id=(dp, target, col), device_id_type=MESH,
        )
        copy.start()
        return copy

    feats = []
    passing = rows == 4
    if passing:
        beside = row + 1 - 2 * lax.rem(row, 2)
        across = row + 2 - 4 * (row // 2)
        size = tile // 2
        ends = [feat_ref.at[pl.ds(part * size, size)] for part in range(2)]
        feats.append(send_block(ends[0], row, 0, 2, beside, 0))
        feats.append(send_block(ends[1], row, 1, 2, across, 2))
        feats.append(send_block(ends[1], row, 1, 2, beside, 1))
        feats.append(send_block(ends[0], row, 0, 2, across, 3))
    else:
        for step in range(1, rows):
            feats.append(send_block(feat_ref, row, 0, 1, row_peer(step), step - 1))

    copies = {}
    numbered = [
        ("low", low_ref, low_in),
        ("feat", feat_ref, gathered.at[pl.ds(pl.multiple_of(row * tile, 16), tile)]),
        ("proj", proj_ref, proj),
        ("conv1", conv1_ref, conv1),
        ("conv2", conv2_ref, conv2),
        ("lwindow", lwindow_ref, lwindow),
    ]
    kind = jnp.where(row == 0, 0, jnp.where(row == rows - 1, 2, 1)) * 3 + jnp.where(
        col == 0, 0, jnp.where(col == cols - 1, 2, 1)
    )
    numbered.append(("up_own", up_own_ref.at[kind], up_own))
    numbered.append(("up_side", up_side_ref.at[kind], up_side))
    for place, (number, tap) in enumerate(plan.taps):
        for slot, j in enumerate((0, 2, 1)):
            numbered.append((
                ("tap", place, slot), atrous_ref.at[number, tap, j],
                weights.at[place, pl.ds(slot * own, own)],
            ))
        if tap == 1 and number < 2:
            numbered.append((
                ("tap", place, 3), (point_ref, pool_ref)[number], weights.at[place, pl.ds(3 * own, own)]
            ))
        else:
            weights[place, pl.ds(3 * own, own), :] = jnp.zeros((own, depth), BF16)
    for place, (name, src, dst) in enumerate(numbered):
        copies[name] = pltpu.make_async_copy(src, dst, local_sem.at[place])
        copies[name].start()

    def pass_on():
        if passing:
            feats[0].wait_recv()
            feats.append(send_block(gathered.at[block(beside, 0, 2)], beside, 0, 2, across, 4))
            feats[1].wait_recv()
            feats.append(send_block(gathered.at[block(across, 1, 2)], across, 1, 2, beside, 5))

    for half_number in range(2):
        empty = jnp.zeros((plan.lead, 2 * own), BF16)
        branches[half_number, 0, pl.ds(0, plan.lead), :] = empty
        branches[half_number, rows - 1, pl.ds(plan.lead + tile, plan.lead), :] = empty
    sums[...] = jnp.zeros(sums.shape, F32)
    distances = [rate // tc for rate in RATES]
    for number, far in enumerate(distances):
        @pl.when(col < far)
        def _():
            zrecv[number, 0] = jnp.zeros(zrecv.shape[2:], BF16)

        @pl.when(col + far >= cols)
        def _():
            zrecv[number, 1] = jnp.zeros(zrecv.shape[2:], BF16)

    low_ends = (pl.ds(0, plan.lhalo), pl.ds(plan.low - plan.lhalo, plan.lhalo))
    low_sides = (pl.ds(plan.low, plan.lstrip), pl.ds(plan.low + plan.lstrip, plan.lstrip))
    for side, edge in ((0, row == 0), (1, row == rows - 1)):
        @pl.when(edge)
        def _():
            low_all[low_ends[side], :] = jnp.zeros((plan.lhalo, low_all.shape[1]), BF16)

    for side, edge in ((0, col == 0), (1, col == cols - 1)):
        @pl.when(edge)
        def _():
            low_all[low_sides[side], :] = jnp.zeros((plan.lstrip, low_all.shape[1]), BF16)
            crecv[side] = jnp.zeros(crecv.shape[1:], BF16)

    def pair(refs, sends, recvs, along):
        made = []
        for side in range(2):
            src, dst = refs[side]
            step = -1 if side == 0 else 1
            if along == "row":
                there = row + step >= 0 if side == 0 else row + step < rows
                target = (dp, lax.rem(row + step + rows, rows), col)
            else:
                there = col + step >= 0 if side == 0 else col + step < cols
                target = (dp, row, lax.rem(col + step + cols, cols))
            made.append((there, pltpu.make_async_remote_copy(
                src_ref=src, dst_ref=dst, send_sem=sends.at[side], recv_sem=recvs.at[1 - side],
                device_id=target, device_id_type=MESH,
            ), recvs.at[side], refs[1 - side][1]))
        return made

    def start_pair(made):
        for there, copy, _, _ in made:
            @pl.when(there)
            def _():
                copy.start()

    def wait_recv_pair(made):
        for there, copy, sem, landed in made:
            @pl.when(there)
            def _():
                pltpu.make_async_copy(landed, landed, sem).wait()

    def wait_send_pair(made):
        for there, copy, _, _ in made:
            @pl.when(there)
            def _():
                copy.wait_send()

    def multiply(owner, number):
        for place, (which, tap) in enumerate(plan.taps):
            if which != number:
                continue
            offset = (tap - 1) * RATES[number]
            whole, rest = offset // plan.tr, offset % plan.tr
            used = [whole, whole + 1] if rest else [whole]

            def add(step, value):
                to = owner - step

                def body():
                    sums[number, block(to), :] += value

                if step == 0:
                    body()
                else:
                    pl.when((to >= 0) & (to < rows))(body)

            def body():
                term = dot_t(gathered[block(owner), :], weights[place])
                if rest:
                    term = term.reshape(tile // plan.tr, plan.tr, 4 * own)
                    term = pltpu.roll(term, plan.tr - rest, 1)
                    upper = lax.broadcasted_iota(jnp.int32, term.shape, 1) < plan.tr - rest
                    terms = [jnp.where(upper, term, 0.0), jnp.where(upper, 0.0, term)]
                    terms = [value.reshape(tile, 4 * own) for value in terms]
                else:
                    terms = [term]
                for step, value in zip(used, terms):
                    add(step, value)

            if offset == 0:
                body()
            else:
                pl.when((owner - used[0] >= 0) & (owner - used[-1] < rows))(body)

    def multiply_own():
        copies["feat"].wait()
        for name, copy in copies.items():
            if name[0] == "tap":
                copy.wait()
        for number in range(3):
            multiply(row, number)

    if passing:
        arrivals = [(beside, (2,)), (across, (3,)), (rows - 1 - row, (4, 5))]
    else:
        arrivals = [(lax.rem(row - step + rows, rows), (step - 1,)) for step in range(1, rows)]

    def multiply_rest():
        for owner, waits in arrivals[:-1]:
            for at in waits:
                feats[at].wait_recv()
            for number in range(3):
                multiply(owner, number)
        for at in arrivals[-1][1]:
            feats[at].wait_recv()

    def last_products(number):
        multiply(arrivals[-1][0], number)

    copies["low"].wait()
    reduced = dot_t(low_in[...], low_weight_ref[...]) + low_bias_ref[...]
    low_all[pl.ds(plan.lhalo, plan.fr * plan.fc), :] = jnp.maximum(reduced, 0.0).astype(BF16)
    low_rows = pair(
        (
            (low_all.at[pl.ds(plan.lhalo, plan.lhalo)], low_all.at[low_ends[1]]),
            (low_all.at[pl.ds(plan.low - 2 * plan.lhalo, plan.lhalo)], low_all.at[low_ends[0]]),
        ),
        lr_send, lr_recv, "row",
    )
    start_pair(low_rows)

    multiply_own()
    pass_on()
    wait_recv_pair(low_rows)
    lsend[...] = dot(lpick_ref[:, pl.ds(0, plan.low)], low_all[pl.ds(0, plan.low), :]).astype(BF16)
    low_cols = pair(
        (
            (lsend.at[pl.ds(0, plan.lstrip)], low_all.at[low_sides[1]]),
            (lsend.at[pl.ds(plan.lstrip, plan.lstrip)], low_all.at[low_sides[0]]),
        ),
        lc_send, lc_recv, "col",
    )
    start_pair(low_cols)

    copies["proj"].wait()
    for w in range(rows):
        for slot, branch in enumerate((0, 3, 1, 2)):
            proj_blocks[w, pl.ds(slot * own, own), :] = proj[
                pl.ds(branch * joined + w * own, own), :
            ]

    wait_recv_pair(low_cols)
    copies["lwindow"].wait()
    copies["conv1"].wait()
    reduced_window[...] = dot(lwindow[:, pl.ds(0, low_all.shape[0])], low_all[...]).astype(BF16)
    wide = conv1.shape[3]
    fine = conv1.shape[2] - low_all.shape[1]
    hidden_px = (plan.wr - 2) * width
    out_px = plan.fr * width
    tail = jnp.zeros((8, wide), F32)
    for j in range(2):
        shifted[j, pl.ds(hidden_px, 8), :] = tail
    for j in range(3):
        total = None
        for i in range(3):
            term = dot(
                reduced_window[pl.ds(i * width, hidden_px), :],
                conv1[i, j, pl.ds(fine, low_all.shape[1]), :],
            )
            total = term if total is None else total + term
        if j == 0:
            low_part[...] = total + conv1_bias_ref[...]
        else:
            shifted[j - 1, pl.ds(0, hidden_px), :] = total
    low_part[...] += shifted[0, pl.ds(1, hidden_px), :] + shifted[1, pl.ds(2, hidden_px), :]

    multiply_rest()

    half = plan.half
    sideways = [None, None, None]
    pool_copies = []
    for number in (2, 1, 0):
        rate = RATES[number]
        last_products(number)
        for side in range(2):
            lanes = pl.ds(side * own, own)
            zsend[number, side] = jnp.concatenate(
                [sums[number, pl.ds(0, half), lanes], sums[number, pl.ds(half, half), lanes]], axis=1
            ).astype(BF16)
        made = []
        for side, far in ((0, distances[number]), (1, -distances[number])):
            there = col + far < cols if far > 0 else col + far >= 0
            come = col - far < cols if far < 0 else col - far >= 0
            copy = pltpu.make_async_remote_copy(
                src_ref=zsend.at[number, side], dst_ref=zrecv.at[number, side],
                send_sem=z_send.at[number, side], recv_sem=z_recv.at[number, side],
                device_id=(dp, row, lax.rem(col + far + 4 * cols, cols)), device_id_type=MESH,
            )
            made.append((there, come, copy))

            @pl.when(there)
            def _():
                copy.start()
        sideways[number] = made
        if number == 1:
            part = jnp.sum(sums[number, :, pl.ds(3 * own, own)], axis=0, keepdims=True)
            pools[col] = jnp.broadcast_to(part, (8, own))
            for step in range(1, cols):
                copy = pltpu.make_async_remote_copy(
                    src_ref=pools.at[col], dst_ref=pools.at[col],
                    send_sem=pool_send.at[step - 1], recv_sem=pool_recv.at[step - 1],
                    device_id=(dp, row, col_peer(step)), device_id_type=MESH,
                )
                copy.start()
                pool_copies.append(copy)

    def bias(number):
        return aspp_bias_ref[pl.ds(number, 1), :]

    def point_branch(part):
        value = sums[0, pl.ds(part * half, half), pl.ds(3 * own, own)]
        return jnp.maximum(value + bias(0), 0.0).astype(BF16)

    def arrive(number):
        for there, come, copy in sideways[number]:
            @pl.when(come)
            def _():
                copy.wait_recv()

    def atrous_branch(number, part):
        lanes = pl.ds(part * own, own)
        value = sums[number, pl.ds(part * half, half), pl.ds(2 * own, own)]
        value = value + zrecv[number, 0, :, lanes].astype(F32) + zrecv[number, 1, :, lanes].astype(F32)
        return jnp.maximum(value + bias(number + 1), 0.0).astype(BF16)

    b_copies = [[], []]

    def send_branches(message, made):
        joint = [jnp.concatenate(made(part), axis=1) for part in range(2)]
        joint = jnp.concatenate(joint, axis=0)
        for place in range(rows):
            value = joint[place * tile:(place + 1) * tile]
            branches[message, place, pl.ds(plan.lead, tile), :] = value
            ends = dot(rpick_ref[:, pl.ds(0, tile)], value).astype(BF16)
            if place + 1 < rows:
                branches[message, place + 1, pl.ds(0, plan.lead), :] = ends[: plan.lead]
            if place > 0:
                branches[message, place - 1, pl.ds(plan.lead + tile, plan.lead), :] = ends[plan.lead:]
        for step in range(1, rows):
            copy = pltpu.make_async_remote_copy(
                src_ref=branches.at[message, row_peer(step)], dst_ref=brecv.at[message, row],
                send_sem=b_send.at[message, step - 1], recv_sem=b_recv.at[message, step - 1],
                device_id=(dp, row_peer(step), col), device_id_type=MESH,
            )
            copy.start()
            b_copies[message].append(copy)
        brecv[message, row] = branches[message, row]

    arrive(2)
    send_branches(0, lambda part: [point_branch(part), atrous_branch(2, part)])

    for copy in pool_copies:
        copy.wait_recv()
    pooled = pools[0]
    for place in range(1, cols):
        pooled = pooled + pools[place]
    pooled = pooled / (plan.height * cols * tc)
    last = jnp.maximum(pooled + aspp_bias_ref[pl.ds(4, 1), :], 0.0)
    branch_pool[row] = jnp.concatenate([last, last], axis=0).astype(BF16)
    bp_copies = []
    for step in range(1, rows):
        copy = pltpu.make_async_remote_copy(
            src_ref=branch_pool.at[row], dst_ref=branch_pool.at[row],
            send_sem=bp_send.at[step - 1], recv_sem=bp_recv.at[step - 1],
            device_id=(dp, row_peer(step), col), device_id_type=MESH,
        )
        copy.start()
        bp_copies.append(copy)

    arrive(1)
    arrive(0)
    send_branches(1, lambda part: [atrous_branch(0, part), atrous_branch(1, part)])

    for copy in bp_copies:
        copy.wait_recv()
    constant = proj_bias_ref[...]
    for w in range(rows):
        constant = constant + dot(
            branch_pool[w], proj[pl.ds(4 * joined + w * own, own), :]
        )[0:1, :]
    coarse = constant
    for message in range(2):
        for copy in b_copies[message]:
            copy.wait_recv()
        for w in range(rows):
            coarse = coarse + dot(
                brecv[message, w], proj_blocks[w, pl.ds(message * 2 * own, 2 * own), :]
            )
    coarse = jnp.maximum(coarse, 0.0).astype(BF16)

    cstrips[...] = dot(cpick_ref[:, pl.ds(0, plan.span)], coarse).astype(BF16)
    coarse_cols = pair(
        (
            (cstrips.at[pl.ds(0, plan.cstrip)], crecv.at[1]),
            (cstrips.at[pl.ds(plan.cstrip, plan.cstrip)], crecv.at[0]),
        ),
        c_send, c_recv, "col",
    )
    start_pair(coarse_cols)
    copies["up_own"].wait()
    copies["up_side"].wait()
    copies["conv2"].wait()
    up_sums = dot(up_own[:, pl.ds(0, plan.span)], coarse)
    wait_recv_pair(coarse_cols)
    strips = jnp.concatenate([crecv[0], crecv[1]], axis=0)
    up_window[...] = (up_sums + dot(up_side[:, pl.ds(0, 2 * plan.cstrip)], strips)).astype(BF16)

    def convolve(source, weight, depth, size):
        wide_in = jnp.concatenate(
            [source[pl.ds(i * width, size), :] for i in range(3)], axis=1
        )
        first = None
        for j in range(3):
            stacked = jnp.concatenate(
                [weight[i, j, pl.ds(0, depth), :] for i in range(3)], axis=0
            )
            total = dot(wide_in, stacked)
            if j == 0:
                first = total
            else:
                shifted[j - 1, pl.ds(0, size), :] = total
        return first + shifted[0, pl.ds(1, size), :] + shifted[1, pl.ds(2, size), :]

    result = convolve(up_window, conv1, fine, hidden_px) + low_part[...]
    result = jnp.maximum(result, 0.0).reshape(plan.wr - 2, width, wide)
    a = lax.broadcasted_iota(jnp.int32, result.shape, 0)
    b = lax.broadcasted_iota(jnp.int32, result.shape, 1)
    low_a = jnp.where(row == 0, 1, 0)
    high_a = jnp.where(row == rows - 1, plan.fr + 1, plan.fr + 2)
    low_b = jnp.where(col == 0, 1, 0)
    high_b = jnp.where(col == cols - 1, plan.fc + 1, plan.fc + 2)
    inside = (a >= low_a) & (a < high_a) & (b >= low_b) & (b < high_b)
    result = jnp.where(inside, result, 0.0)
    hidden[...] = result.reshape(hidden_px, wide).astype(BF16)

    result = convolve(hidden, conv2, conv2.shape[2], out_px) + conv2_bias_ref[...]
    result = jnp.maximum(result, 0.0).reshape(plan.fr, width, wide)
    out_ref[...] = result[:, : plan.fc, :].astype(BF16)

    for copy in feats + pool_copies + bp_copies + b_copies[0] + b_copies[1]:
        copy.wait_send()
    for made in sideways:
        for there, come, copy in made:
            @pl.when(there)
            def _():
                copy.wait_send()
    for made in (low_rows, low_cols, coarse_cols):
        wait_send_pair(made)


def on_device(
    plan,
    features, low_level, point_weight, atrous_weight, pool_weight, aspp_bias, proj_weight, proj_bias,
    low_weight, low_bias, conv1_weight, conv1_bias, conv2_weight, conv2_bias,
):
    own, depth = point_weight.shape[::-1]
    out_width = proj_weight.shape[1]
    red = low_weight.shape[1]
    rows, cols = plan.rows, plan.cols
    taps = len(plan.taps)
    wide = conv1_weight.shape[3]
    up_own, up_side = plan.upsample()
    any_spec = pl.BlockSpec(memory_space=pl.ANY)
    vmem = pl.BlockSpec(memory_space=pltpu.VMEM)
    dma = pltpu.SemaphoreType.DMA
    hidden_px = (plan.wr - 2) * plan.width
    feat_sends = 6 if rows == 4 else rows - 1
    scratch = [
        pltpu.VMEM((plan.pixels, depth), BF16),
        pltpu.VMEM((taps, 4 * own, depth), BF16),
        pltpu.VMEM((plan.fr * plan.fc, low_level.shape[2]), BF16),
        pltpu.VMEM(proj_weight.shape, BF16),
        pltpu.VMEM(conv1_weight.shape, BF16),
        pltpu.VMEM(conv2_weight.shape, BF16),
        pltpu.VMEM(up_own.shape[1:], BF16),
        pltpu.VMEM(up_side.shape[1:], BF16),
        pltpu.VMEM(plan.low_window().shape, BF16),
        pltpu.VMEM((3, plan.pixels, 4 * own), F32),
        pltpu.VMEM((3, 2, plan.half, 2 * own), BF16),
        pltpu.VMEM((3, 2, plan.half, 2 * own), BF16),
        pltpu.VMEM((cols, 8, own), F32),
        pltpu.VMEM((rows, 16, own), BF16),
        pltpu.VMEM((2, rows, plan.span, 2 * own), BF16),
        pltpu.VMEM((2, rows, plan.span, 2 * own), BF16),
        pltpu.VMEM((rows, 4 * own, out_width), BF16),
        pltpu.VMEM((2 * plan.cstrip, out_width), BF16),
        pltpu.VMEM((2, plan.cstrip, out_width), BF16),
        pltpu.VMEM((plan.low + 2 * plan.lstrip, red), BF16),
        pltpu.VMEM((2 * plan.lstrip, red), BF16),
        pltpu.VMEM((plan.window, red), BF16),
        pltpu.VMEM((2, hidden_px + 8, wide), F32),
        pltpu.VMEM((hidden_px, wide), F32),
        pltpu.VMEM((plan.window, out_width), BF16),
        pltpu.VMEM((hidden_px, wide), BF16),
        dma((8 + 4 * taps,)),
        dma((feat_sends,)), dma((feat_sends,)),
        dma((3, 2)), dma((3, 2)),
        dma((cols - 1,)), dma((cols - 1,)),
        dma((rows - 1,)), dma((rows - 1,)),
        dma((2, rows - 1)), dma((2, rows - 1)),
        dma((2,)), dma((2,)), dma((2,)), dma((2,)), dma((2,)), dma((2,)),
    ]
    return pl.pallas_call(
        functools.partial(kernel, plan),
        out_shape=jax.ShapeDtypeStruct((plan.fr, plan.fc, wide), BF16),
        in_specs=[
            any_spec, any_spec, any_spec, any_spec, any_spec, vmem, any_spec, vmem,
            vmem, vmem, any_spec, vmem, any_spec, vmem,
            any_spec, any_spec, vmem, vmem, vmem, any_spec,
        ],
        out_specs=vmem,
        scratch_shapes=scratch,
        compiler_params=pltpu.CompilerParams(
            collective_id=0, has_side_effects=True, vmem_limit_bytes=60 * 1024 * 1024
        ),
    )(
        jnp.transpose(features, (1, 0, 2)).reshape(plan.tile, depth),
        low_level.reshape(plan.fr * plan.fc, low_level.shape[2]),
        point_weight.T, jnp.swapaxes(atrous_weight, 3, 4), pool_weight.T, aspp_bias, proj_weight,
        proj_bias[None], low_weight.T, low_bias[None], conv1_weight, conv1_bias[None], conv2_weight, conv2_bias[None],
        jnp.asarray(up_own, BF16), jnp.asarray(up_side, BF16),
        jnp.asarray(plan.row_strips(), BF16), jnp.asarray(plan.coarse_strips(), BF16), jnp.asarray(plan.low_strips(), BF16),
        jnp.asarray(plan.low_window(), BF16),
    )


def solution(mesh):
    placed = (
        P(("dp", "row"), "col", None),
        P(("dp", "row"), "col", None),
        P(None, "row"),
        P(None, None, None, None, "row"),
        P(None, "row"),
        P(None, "row"),
        P(),
        P(),
        P(),
        P(),
        P(),
        P(),
        P(),
        P(),
    )

    def local(features, *others):
        plan = Plan(mesh.shape["row"], mesh.shape["col"], features.shape[0], features.shape[1])
        return on_device(plan, features, *others)

    return jax.shard_map(
        local,
        mesh=mesh,
        in_specs=placed,
        out_specs=P(("dp", "row"), "col", None),
        check_vma=False,
    )
```

```python
import functools

import jax
import jax.numpy as jnp
import numpy as np
from jax import lax
from jax.experimental import pallas as pl
from jax.experimental.pallas import tpu as pltpu
from jax.sharding import PartitionSpec as P

RATES = (12, 24, 36)
MESH = pl.DeviceIdType.MESH
F32 = jnp.float32
BF16 = jnp.bfloat16


def up16(value):
    return -(-value // 16) * 16


def table(values):
    lanes = -values.shape[-1] % 128
    return np.pad(values, [(0, 0)] * (values.ndim - 1) + [(0, lanes)])


class Plan:
    def __init__(self, rows, cols, tile_rows, tile_cols):
        self.rows, self.cols = rows, cols
        self.tr, self.tc = tile_rows, tile_cols
        self.tile = tile_rows * tile_cols
        self.height = rows * tile_rows
        self.pixels = self.height * tile_cols
        self.half = self.pixels // 2
        self.lead = up16(2 * tile_cols)
        self.span = self.tile + 2 * self.lead
        self.cstrip = up16((tile_rows + 4) * 2)
        self.fr, self.fc = 2 * tile_rows, 2 * tile_cols
        self.wr, self.wc = self.fr + 4, self.fc + 4
        self.width = 32 * (-(-self.wc // 32))
        self.window = self.wr * self.width
        self.lhalo = 2 * self.fc
        self.low = self.wr * self.fc
        self.lstrip = up16(self.wr * 2)
        self.taps = []
        for number, rate in enumerate(RATES):
            for tap in range(3):
                if abs(tap - 1) * rate < self.height:
                    self.taps.append((number, tap))

    def upsample(self):
        own = np.zeros((9, self.window, self.span), np.float32)
        side = np.zeros((9, self.window, 2 * self.cstrip), np.float32)

        def terms(fine, length, first, last):
            if (first and fine < 0) or (last and fine >= 2 * length):
                return []
            middle = fine // 2
            other = middle - 1 if fine % 2 == 0 else middle + 1
            found = []
            for place, weight in ((middle, 0.75), (other, 0.25)):
                place = max(place, 0) if first else place
                place = min(place, length - 1) if last else place
                found.append((place, weight))
            return found

        for kind in range(9):
            top, bottom = kind // 3 == 0, kind // 3 == 2
            left, right = kind % 3 == 0, kind % 3 == 2
            for a in range(self.wr):
                for b in range(self.wc):
                    at = a * self.width + b
                    for y, wy in terms(a - 2, self.tr, top, bottom):
                        for x, wx in terms(b - 2, self.tc, left, right):
                            if x < 0:
                                side[kind, at, (y + 2) * 2 + x + 2] += wy * wx
                            elif x >= self.tc:
                                side[kind, at, self.cstrip + (y + 2) * 2 + x - self.tc] += wy * wx
                            else:
                                own[kind, at, self.pixel(y, x)] += wy * wx
        return table(own), table(side)

    def pixel(self, y, x):
        if y < 0:
            return x * 2 + y + 2
        if y >= self.tr:
            return self.lead + self.tile + x * 2 + y - self.tr
        return self.lead + x * self.tr + y

    def row_strips(self):
        pick = np.zeros((2 * self.lead, self.tile), np.float32)
        for x in range(self.tc):
            for y in range(2):
                pick[x * 2 + y, x * self.tr + self.tr - 2 + y] = 1
                pick[self.lead + x * 2 + y, x * self.tr + y] = 1
        return table(pick)

    def coarse_strips(self):
        pick = np.zeros((2 * self.cstrip, self.span), np.float32)
        for y in range(-2, self.tr + 2):
            for x in range(2):
                pick[(y + 2) * 2 + x, self.pixel(y, x)] = 1
                pick[self.cstrip + (y + 2) * 2 + x, self.pixel(y, self.tc - 2 + x)] = 1
        return table(pick)

    def low_strips(self):
        pick = np.zeros((2 * self.lstrip, self.low), np.float32)
        for y in range(self.wr):
            for x in range(2):
                pick[y * 2 + x, y * self.fc + x] = 1
                pick[self.lstrip + y * 2 + x, y * self.fc + self.fc - 2 + x] = 1
        return table(pick)

    def low_window(self):
        pick = np.zeros((self.window, self.low + 2 * self.lstrip), np.float32)
        for y in range(self.wr):
            for b in range(self.wc):
                x = b - 2
                if x < 0:
                    place = self.low + y * 2 + b
                elif x >= self.fc:
                    place = self.low + self.lstrip + y * 2 + x - self.fc
                else:
                    place = y * self.fc + x
                pick[y * self.width + b, place] = 1
        return table(pick)


def dot(a, b):
    return jnp.dot(a, b, preferred_element_type=F32)


def dot_t(a, b):
    return lax.dot_general(a, b, (((1,), (1,)), ((), ())), preferred_element_type=F32)


def kernel(
    plan,
    feat_ref, low_ref, point_ref, atrous_ref, pool_ref, aspp_bias_ref, proj_ref, proj_bias_ref,
    low_weight_ref, low_bias_ref, conv1_ref, conv1_bias_ref, conv2_ref, conv2_bias_ref,
    up_own_ref, up_side_ref, rpick_ref, cpick_ref, lpick_ref, lwindow_ref,
    out_ref,
    gathered, weights, turned, low_in, proj, conv1, conv2, up_own, up_side, lwindow,
    sums, zsend, zrecv, pools, branch_pool, branches, brecv, proj_blocks,
    cstrips, crecv, low_all, lsend, reduced_window, shifted, low_part, up_window, hidden,
    local_sem, feat_send, feat_recv, z_send, z_recv, pool_send, pool_recv, bp_send, bp_recv,
    b_send, b_recv, c_send, c_recv, lr_send, lr_recv, lc_send, lc_recv,
):
    rows, cols = plan.rows, plan.cols
    tile, tc, width = plan.tile, plan.tc, plan.width
    dp, row, col = lax.axis_index("dp"), lax.axis_index("row"), lax.axis_index("col")
    own, depth = point_ref.shape
    joined = own * rows

    def row_peer(step):
        return lax.rem(row + step, rows)

    def col_peer(step):
        return lax.rem(col + step, cols)

    barrier = pltpu.get_barrier_semaphore()
    for step in range(1, rows):
        pl.semaphore_signal(barrier, inc=1, device_id=(dp, row_peer(step), col), device_id_type=MESH)
    for step in range(1, cols):
        pl.semaphore_signal(barrier, inc=1, device_id=(dp, row, col_peer(step)), device_id_type=MESH)
    pl.semaphore_wait(barrier, rows + cols - 2)

    def block(owner, part=0, parts=1):
        size = tile // parts
        return pl.ds(pl.multiple_of(owner * tile + part * size, 16), size)

    def send_block(src, owner, part, parts, target, at):
        copy = pltpu.make_async_remote_copy(
            src_ref=src, dst_ref=gathered.at[block(owner, part, parts)],
            send_sem=feat_send.at[at], recv_sem=feat_recv.at[at],
            device_id=(dp, target, col), device_id_type=MESH,
        )
        copy.start()
        return copy

    feats = []
    passing = rows == 4
    if passing:
        beside = row + 1 - 2 * lax.rem(row, 2)
        across = row + 2 - 4 * (row // 2)
        size = tile // 2
        ends = [feat_ref.at[pl.ds(part * size, size)] for part in range(2)]
        feats.append(send_block(ends[0], row, 0, 2, beside, 0))
        feats.append(send_block(ends[1], row, 1, 2, across, 2))
        feats.append(send_block(ends[1], row, 1, 2, beside, 1))
        feats.append(send_block(ends[0], row, 0, 2, across, 3))
    else:
        for step in range(1, rows):
            feats.append(send_block(feat_ref, row, 0, 1, row_peer(step), step - 1))

    copies = {}
    numbered = [
        ("low", low_ref, low_in),
        ("feat", feat_ref, gathered.at[pl.ds(pl.multiple_of(row * tile, 16), tile)]),
        ("proj", proj_ref, proj),
        ("conv1", conv1_ref, conv1),
        ("conv2", conv2_ref, conv2),
        ("lwindow", lwindow_ref, lwindow),
    ]
    kind = jnp.where(row == 0, 0, jnp.where(row == rows - 1, 2, 1)) * 3 + jnp.where(
        col == 0, 0, jnp.where(col == cols - 1, 2, 1)
    )
    numbered.append(("up_own", up_own_ref.at[kind], up_own))
    numbered.append(("up_side", up_side_ref.at[kind], up_side))
    for place, (number, tap) in enumerate(plan.taps):
        for slot, j in enumerate((0, 2, 1)):
            numbered.append((
                ("tap", place, slot), atrous_ref.at[number, tap, j],
                weights.at[place, pl.ds(slot * own, own)],
            ))
        if tap == 1 and number < 2:
            numbered.append((
                ("tap", place, 3), (point_ref, pool_ref)[number], weights.at[place, pl.ds(3 * own, own)]
            ))
        else:
            weights[place, pl.ds(3 * own, own), :] = jnp.zeros((own, depth), BF16)
    for place, (name, src, dst) in enumerate(numbered):
        copies[name] = pltpu.make_async_copy(src, dst, local_sem.at[place])
        copies[name].start()

    def pass_on():
        if passing:
            feats[0].wait_recv()
            feats.append(send_block(gathered.at[block(beside, 0, 2)], beside, 0, 2, across, 4))
            feats[1].wait_recv()
            feats.append(send_block(gathered.at[block(across, 1, 2)], across, 1, 2, beside, 5))

    for half_number in range(2):
        empty = jnp.zeros((plan.lead, 2 * own), BF16)
        branches[half_number, 0, pl.ds(0, plan.lead), :] = empty
        branches[half_number, rows - 1, pl.ds(plan.lead + tile, plan.lead), :] = empty
    distances = [rate // tc for rate in RATES]
    for number, far in enumerate(distances):
        @pl.when(col < far)
        def _():
            zrecv[number, 0] = jnp.zeros(zrecv.shape[2:], BF16)

        @pl.when(col + far >= cols)
        def _():
            zrecv[number, 1] = jnp.zeros(zrecv.shape[2:], BF16)

    low_ends = (pl.ds(0, plan.lhalo), pl.ds(plan.low - plan.lhalo, plan.lhalo))
    low_sides = (pl.ds(plan.low, plan.lstrip), pl.ds(plan.low + plan.lstrip, plan.lstrip))
    for side, edge in ((0, row == 0), (1, row == rows - 1)):
        @pl.when(edge)
        def _():
            low_all[low_ends[side], :] = jnp.zeros((plan.lhalo, low_all.shape[1]), BF16)

    for side, edge in ((0, col == 0), (1, col == cols - 1)):
        @pl.when(edge)
        def _():
            low_all[low_sides[side], :] = jnp.zeros((plan.lstrip, low_all.shape[1]), BF16)
            crecv[side] = jnp.zeros(crecv.shape[1:], BF16)

    def pair(refs, sends, recvs, along):
        made = []
        for side in range(2):
            src, dst = refs[side]
            step = -1 if side == 0 else 1
            if along == "row":
                there = row + step >= 0 if side == 0 else row + step < rows
                target = (dp, lax.rem(row + step + rows, rows), col)
            else:
                there = col + step >= 0 if side == 0 else col + step < cols
                target = (dp, row, lax.rem(col + step + cols, cols))
            made.append((there, pltpu.make_async_remote_copy(
                src_ref=src, dst_ref=dst, send_sem=sends.at[side], recv_sem=recvs.at[1 - side],
                device_id=target, device_id_type=MESH,
            ), recvs.at[side], refs[1 - side][1]))
        return made

    def start_pair(made):
        for there, copy, _, _ in made:
            @pl.when(there)
            def _():
                copy.start()

    def wait_recv_pair(made):
        for there, copy, sem, landed in made:
            @pl.when(there)
            def _():
                pltpu.make_async_copy(landed, landed, sem).wait()

    def wait_send_pair(made):
        for there, copy, _, _ in made:
            @pl.when(there)
            def _():
                copy.wait_send()

    piece = min(256, depth)

    def turn_weights():
        for name, copy in copies.items():
            if name[0] == "tap":
                copy.wait()
        for place in range(len(plan.taps)):
            for begin in range(0, depth, piece):
                turned[place, pl.ds(begin, piece), :] = weights[place, :, pl.ds(begin, piece)].T

    def products(number):
        for place, (which, tap) in enumerate(plan.taps):
            if which == number and tap == 1:
                sums[number] = dot(gathered[...], turned[place])
        for place, (which, tap) in enumerate(plan.taps):
            if which == number and tap != 1:
                offset = (tap - 1) * RATES[number]
                whole, rest = offset // plan.tr, offset % plan.tr
                used = [whole, whole + 1] if rest else [whole]
                first = max(0, used[0])
                final = min(rows, rows + used[-1])
                size = (final - first) * tile
                term = dot(gathered[pl.ds(first * tile, size), :], turned[place])
                if rest:
                    term = term.reshape(size // plan.tr, plan.tr, 4 * own)
                    term = pltpu.roll(term, plan.tr - rest, 1)
                    upper = lax.broadcasted_iota(jnp.int32, term.shape, 1) < plan.tr - rest
                    terms = [jnp.where(upper, term, 0.0), jnp.where(upper, 0.0, term)]
                    terms = [value.reshape(size, 4 * own) for value in terms]
                else:
                    terms = [term]
                for step, value in zip(used, terms):
                    begin, end = max(0, -step), min(rows, rows - step)
                    count = (end - begin) * tile
                    if count > 0:
                        skip = (begin + step - first) * tile
                        sums[number, pl.ds(begin * tile, count), :] += value[skip:skip + count]

    copies["low"].wait()
    reduced = dot_t(low_in[...], low_weight_ref[...]) + low_bias_ref[...]
    low_all[pl.ds(plan.lhalo, plan.fr * plan.fc), :] = jnp.maximum(reduced, 0.0).astype(BF16)
    low_rows = pair(
        (
            (low_all.at[pl.ds(plan.lhalo, plan.lhalo)], low_all.at[low_ends[1]]),
            (low_all.at[pl.ds(plan.low - 2 * plan.lhalo, plan.lhalo)], low_all.at[low_ends[0]]),
        ),
        lr_send, lr_recv, "row",
    )
    start_pair(low_rows)

    turn_weights()
    pass_on()
    wait_recv_pair(low_rows)
    lsend[...] = dot(lpick_ref[:, pl.ds(0, plan.low)], low_all[pl.ds(0, plan.low), :]).astype(BF16)
    low_cols = pair(
        (
            (lsend.at[pl.ds(0, plan.lstrip)], low_all.at[low_sides[1]]),
            (lsend.at[pl.ds(plan.lstrip, plan.lstrip)], low_all.at[low_sides[0]]),
        ),
        lc_send, lc_recv, "col",
    )
    start_pair(low_cols)

    copies["proj"].wait()
    for w in range(rows):
        for slot, branch in enumerate((0, 3, 1, 2)):
            proj_blocks[w, pl.ds(slot * own, own), :] = proj[
                pl.ds(branch * joined + w * own, own), :
            ]

    wait_recv_pair(low_cols)
    copies["lwindow"].wait()
    copies["conv1"].wait()
    reduced_window[...] = dot(lwindow[:, pl.ds(0, low_all.shape[0])], low_all[...]).astype(BF16)
    wide = conv1.shape[3]
    fine = conv1.shape[2] - low_all.shape[1]
    hidden_px = (plan.wr - 2) * width
    out_px = plan.fr * width
    tail = jnp.zeros((8, wide), F32)
    for j in range(2):
        shifted[j, pl.ds(hidden_px, 8), :] = tail
    for j in range(3):
        total = None
        for i in range(3):
            term = dot(
                reduced_window[pl.ds(i * width, hidden_px), :],
                conv1[i, j, pl.ds(fine, low_all.shape[1]), :],
            )
            total = term if total is None else total + term
        if j == 0:
            low_part[...] = total + conv1_bias_ref[...]
        else:
            shifted[j - 1, pl.ds(0, hidden_px), :] = total
    low_part[...] += shifted[0, pl.ds(1, hidden_px), :] + shifted[1, pl.ds(2, hidden_px), :]

    copies["feat"].wait()
    for copy in feats[2 if passing else 0:]:
        copy.wait_recv()

    half = plan.half
    sideways = [None, None, None]
    pool_copies = []
    for number in (2, 1, 0):
        rate = RATES[number]
        products(number)
        for side in range(2):
            lanes = pl.ds(side * own, own)
            zsend[number, side] = jnp.concatenate(
                [sums[number, pl.ds(0, half), lanes], sums[number, pl.ds(half, half), lanes]], axis=1
            ).astype(BF16)
        made = []
        for side, far in ((0, distances[number]), (1, -distances[number])):
            there = col + far < cols if far > 0 else col + far >= 0
            come = col - far < cols if far < 0 else col - far >= 0
            copy = pltpu.make_async_remote_copy(
                src_ref=zsend.at[number, side], dst_ref=zrecv.at[number, side],
                send_sem=z_send.at[number, side], recv_sem=z_recv.at[number, side],
                device_id=(dp, row, lax.rem(col + far + 4 * cols, cols)), device_id_type=MESH,
            )
            made.append((there, come, copy))

            @pl.when(there)
            def _():
                copy.start()
        sideways[number] = made
        if number == 1:
            part = jnp.sum(sums[number, :, pl.ds(3 * own, own)], axis=0, keepdims=True)
            pools[col] = jnp.broadcast_to(part, (8, own))
            for step in range(1, cols):
                copy = pltpu.make_async_remote_copy(
                    src_ref=pools.at[col], dst_ref=pools.at[col],
                    send_sem=pool_send.at[step - 1], recv_sem=pool_recv.at[step - 1],
                    device_id=(dp, row, col_peer(step)), device_id_type=MESH,
                )
                copy.start()
                pool_copies.append(copy)

    def bias(number):
        return aspp_bias_ref[pl.ds(number, 1), :]

    def point_branch(part):
        value = sums[0, pl.ds(part * half, half), pl.ds(3 * own, own)]
        return jnp.maximum(value + bias(0), 0.0).astype(BF16)

    def arrive(number):
        for there, come, copy in sideways[number]:
            @pl.when(come)
            def _():
                copy.wait_recv()

    def atrous_branch(number, part):
        lanes = pl.ds(part * own, own)
        value = sums[number, pl.ds(part * half, half), pl.ds(2 * own, own)]
        value = value + zrecv[number, 0, :, lanes].astype(F32) + zrecv[number, 1, :, lanes].astype(F32)
        return jnp.maximum(value + bias(number + 1), 0.0).astype(BF16)

    b_copies = [[], []]

    def send_branches(message, made):
        joint = [jnp.concatenate(made(part), axis=1) for part in range(2)]
        joint = jnp.concatenate(joint, axis=0)
        for place in range(rows):
            value = joint[place * tile:(place + 1) * tile]
            branches[message, place, pl.ds(plan.lead, tile), :] = value
            ends = dot(rpick_ref[:, pl.ds(0, tile)], value).astype(BF16)
            if place + 1 < rows:
                branches[message, place + 1, pl.ds(0, plan.lead), :] = ends[: plan.lead]
            if place > 0:
                branches[message, place - 1, pl.ds(plan.lead + tile, plan.lead), :] = ends[plan.lead:]
        for step in range(1, rows):
            copy = pltpu.make_async_remote_copy(
                src_ref=branches.at[message, row_peer(step)], dst_ref=brecv.at[message, row],
                send_sem=b_send.at[message, step - 1], recv_sem=b_recv.at[message, step - 1],
                device_id=(dp, row_peer(step), col), device_id_type=MESH,
            )
            copy.start()
            b_copies[message].append(copy)
        brecv[message, row] = branches[message, row]

    arrive(2)
    send_branches(0, lambda part: [point_branch(part), atrous_branch(2, part)])

    for copy in pool_copies:
        copy.wait_recv()
    pooled = pools[0]
    for place in range(1, cols):
        pooled = pooled + pools[place]
    pooled = pooled / (plan.height * cols * tc)
    last = jnp.maximum(pooled + aspp_bias_ref[pl.ds(4, 1), :], 0.0)
    branch_pool[row] = jnp.concatenate([last, last], axis=0).astype(BF16)
    bp_copies = []
    for step in range(1, rows):
        copy = pltpu.make_async_remote_copy(
            src_ref=branch_pool.at[row], dst_ref=branch_pool.at[row],
            send_sem=bp_send.at[step - 1], recv_sem=bp_recv.at[step - 1],
            device_id=(dp, row_peer(step), col), device_id_type=MESH,
        )
        copy.start()
        bp_copies.append(copy)

    arrive(1)
    arrive(0)
    send_branches(1, lambda part: [atrous_branch(0, part), atrous_branch(1, part)])

    for copy in bp_copies:
        copy.wait_recv()
    constant = proj_bias_ref[...]
    for w in range(rows):
        constant = constant + dot(
            branch_pool[w], proj[pl.ds(4 * joined + w * own, own), :]
        )[0:1, :]
    coarse = constant
    for message in range(2):
        for copy in b_copies[message]:
            copy.wait_recv()
        for w in range(rows):
            coarse = coarse + dot(
                brecv[message, w], proj_blocks[w, pl.ds(message * 2 * own, 2 * own), :]
            )
    coarse = jnp.maximum(coarse, 0.0).astype(BF16)

    cstrips[...] = dot(cpick_ref[:, pl.ds(0, plan.span)], coarse).astype(BF16)
    coarse_cols = pair(
        (
            (cstrips.at[pl.ds(0, plan.cstrip)], crecv.at[1]),
            (cstrips.at[pl.ds(plan.cstrip, plan.cstrip)], crecv.at[0]),
        ),
        c_send, c_recv, "col",
    )
    start_pair(coarse_cols)
    copies["up_own"].wait()
    copies["up_side"].wait()
    copies["conv2"].wait()
    up_sums = dot(up_own[:, pl.ds(0, plan.span)], coarse)
    wait_recv_pair(coarse_cols)
    strips = jnp.concatenate([crecv[0], crecv[1]], axis=0)
    up_window[...] = (up_sums + dot(up_side[:, pl.ds(0, 2 * plan.cstrip)], strips)).astype(BF16)

    def convolve(source, weight, depth, size):
        wide_in = jnp.concatenate(
            [source[pl.ds(i * width, size), :] for i in range(3)], axis=1
        )
        first = None
        for j in range(3):
            stacked = jnp.concatenate(
                [weight[i, j, pl.ds(0, depth), :] for i in range(3)], axis=0
            )
            total = dot(wide_in, stacked)
            if j == 0:
                first = total
            else:
                shifted[j - 1, pl.ds(0, size), :] = total
        return first + shifted[0, pl.ds(1, size), :] + shifted[1, pl.ds(2, size), :]

    result = convolve(up_window, conv1, fine, hidden_px) + low_part[...]
    result = jnp.maximum(result, 0.0).reshape(plan.wr - 2, width, wide)
    a = lax.broadcasted_iota(jnp.int32, result.shape, 0)
    b = lax.broadcasted_iota(jnp.int32, result.shape, 1)
    low_a = jnp.where(row == 0, 1, 0)
    high_a = jnp.where(row == rows - 1, plan.fr + 1, plan.fr + 2)
    low_b = jnp.where(col == 0, 1, 0)
    high_b = jnp.where(col == cols - 1, plan.fc + 1, plan.fc + 2)
    inside = (a >= low_a) & (a < high_a) & (b >= low_b) & (b < high_b)
    result = jnp.where(inside, result, 0.0)
    hidden[...] = result.reshape(hidden_px, wide).astype(BF16)

    result = convolve(hidden, conv2, conv2.shape[2], out_px) + conv2_bias_ref[...]
    result = jnp.maximum(result, 0.0).reshape(plan.fr, width, wide)
    out_ref[...] = result[:, : plan.fc, :].astype(BF16)

    for copy in feats + pool_copies + bp_copies + b_copies[0] + b_copies[1]:
        copy.wait_send()
    for made in sideways:
        for there, come, copy in made:
            @pl.when(there)
            def _():
                copy.wait_send()
    for made in (low_rows, low_cols, coarse_cols):
        wait_send_pair(made)


def on_device(
    plan,
    features, low_level, point_weight, atrous_weight, pool_weight, aspp_bias, proj_weight, proj_bias,
    low_weight, low_bias, conv1_weight, conv1_bias, conv2_weight, conv2_bias,
):
    own, depth = point_weight.shape[::-1]
    out_width = proj_weight.shape[1]
    red = low_weight.shape[1]
    rows, cols = plan.rows, plan.cols
    taps = len(plan.taps)
    wide = conv1_weight.shape[3]
    up_own, up_side = plan.upsample()
    any_spec = pl.BlockSpec(memory_space=pl.ANY)
    vmem = pl.BlockSpec(memory_space=pltpu.VMEM)
    dma = pltpu.SemaphoreType.DMA
    hidden_px = (plan.wr - 2) * plan.width
    feat_sends = 6 if rows == 4 else rows - 1
    scratch = [
        pltpu.VMEM((plan.pixels, depth), BF16),
        pltpu.VMEM((taps, 4 * own, depth), BF16),
        pltpu.VMEM((taps, depth, 4 * own), BF16),
        pltpu.VMEM((plan.fr * plan.fc, low_level.shape[2]), BF16),
        pltpu.VMEM(proj_weight.shape, BF16),
        pltpu.VMEM(conv1_weight.shape, BF16),
        pltpu.VMEM(conv2_weight.shape, BF16),
        pltpu.VMEM(up_own.shape[1:], BF16),
        pltpu.VMEM(up_side.shape[1:], BF16),
        pltpu.VMEM(plan.low_window().shape, BF16),
        pltpu.VMEM((3, plan.pixels, 4 * own), F32),
        pltpu.VMEM((3, 2, plan.half, 2 * own), BF16),
        pltpu.VMEM((3, 2, plan.half, 2 * own), BF16),
        pltpu.VMEM((cols, 8, own), F32),
        pltpu.VMEM((rows, 16, own), BF16),
        pltpu.VMEM((2, rows, plan.span, 2 * own), BF16),
        pltpu.VMEM((2, rows, plan.span, 2 * own), BF16),
        pltpu.VMEM((rows, 4 * own, out_width), BF16),
        pltpu.VMEM((2 * plan.cstrip, out_width), BF16),
        pltpu.VMEM((2, plan.cstrip, out_width), BF16),
        pltpu.VMEM((plan.low + 2 * plan.lstrip, red), BF16),
        pltpu.VMEM((2 * plan.lstrip, red), BF16),
        pltpu.VMEM((plan.window, red), BF16),
        pltpu.VMEM((2, hidden_px + 8, wide), F32),
        pltpu.VMEM((hidden_px, wide), F32),
        pltpu.VMEM((plan.window, out_width), BF16),
        pltpu.VMEM((hidden_px, wide), BF16),
        dma((8 + 4 * taps,)),
        dma((feat_sends,)), dma((feat_sends,)),
        dma((3, 2)), dma((3, 2)),
        dma((cols - 1,)), dma((cols - 1,)),
        dma((rows - 1,)), dma((rows - 1,)),
        dma((2, rows - 1)), dma((2, rows - 1)),
        dma((2,)), dma((2,)), dma((2,)), dma((2,)), dma((2,)), dma((2,)),
    ]
    return pl.pallas_call(
        functools.partial(kernel, plan),
        out_shape=jax.ShapeDtypeStruct((plan.fr, plan.fc, wide), BF16),
        in_specs=[
            any_spec, any_spec, any_spec, any_spec, any_spec, vmem, any_spec, vmem,
            vmem, vmem, any_spec, vmem, any_spec, vmem,
            any_spec, any_spec, vmem, vmem, vmem, any_spec,
        ],
        out_specs=vmem,
        scratch_shapes=scratch,
        compiler_params=pltpu.CompilerParams(
            collective_id=0, has_side_effects=True, vmem_limit_bytes=60 * 1024 * 1024
        ),
    )(
        jnp.transpose(features, (1, 0, 2)).reshape(plan.tile, depth),
        low_level.reshape(plan.fr * plan.fc, low_level.shape[2]),
        point_weight.T, jnp.swapaxes(atrous_weight, 3, 4), pool_weight.T, aspp_bias, proj_weight,
        proj_bias[None], low_weight.T, low_bias[None], conv1_weight, conv1_bias[None], conv2_weight, conv2_bias[None],
        jnp.asarray(up_own, BF16), jnp.asarray(up_side, BF16),
        jnp.asarray(plan.row_strips(), BF16), jnp.asarray(plan.coarse_strips(), BF16), jnp.asarray(plan.low_strips(), BF16),
        jnp.asarray(plan.low_window(), BF16),
    )


def solution(mesh):
    placed = (
        P(("dp", "row"), "col", None),
        P(("dp", "row"), "col", None),
        P(None, "row"),
        P(None, None, None, None, "row"),
        P(None, "row"),
        P(None, "row"),
        P(),
        P(),
        P(),
        P(),
        P(),
        P(),
        P(),
        P(),
    )

    def local(features, *others):
        plan = Plan(mesh.shape["row"], mesh.shape["col"], features.shape[0], features.shape[1])
        return on_device(plan, features, *others)

    return jax.shard_map(
        local,
        mesh=mesh,
        in_specs=placed,
        out_specs=P(("dp", "row"), "col", None),
        check_vma=False,
    )
```

```python
import functools

import jax
import jax.numpy as jnp
import numpy as np
from jax import lax
from jax.experimental import pallas as pl
from jax.experimental.pallas import tpu as pltpu
from jax.sharding import PartitionSpec as P

RATES = (12, 24, 36)
MESH = pl.DeviceIdType.MESH
F32 = jnp.float32
BF16 = jnp.bfloat16


def up16(value):
    return -(-value // 16) * 16


def table(values):
    lanes = -values.shape[-1] % 128
    return np.pad(values, [(0, 0)] * (values.ndim - 1) + [(0, lanes)])


class Plan:
    def __init__(self, rows, cols, tile_rows, tile_cols):
        self.rows, self.cols = rows, cols
        self.tr, self.tc = tile_rows, tile_cols
        self.tile = tile_rows * tile_cols
        self.height = rows * tile_rows
        self.pc = tile_cols // 2
        self.pt = self.pc * tile_rows
        self.pixels = rows * self.pt
        self.half = self.pixels // 2
        self.lead = up16(2 * self.pc)
        self.span = self.pt + 2 * self.lead
        self.cstrip = up16((tile_rows + 4) * 2)
        self.fr, self.fc = 2 * tile_rows, 2 * tile_cols
        self.wr, self.wc = self.fr + 4, self.fc + 4
        self.width = 32 * (-(-self.wc // 32))
        self.window = self.wr * self.width
        self.lhalo = 2 * self.fc
        self.low = self.wr * self.fc
        self.lstrip = up16(self.wr * 2)
        self.taps = []
        for number, rate in enumerate(RATES):
            for tap in range(3):
                if abs(tap - 1) * rate < self.height:
                    self.taps.append((number, tap))

    def upsample(self):
        own = np.zeros((9, self.window, 2 * self.span), np.float32)
        side = np.zeros((9, self.window, 2 * self.cstrip), np.float32)

        def terms(fine, length, first, last):
            if (first and fine < 0) or (last and fine >= 2 * length):
                return []
            middle = fine // 2
            other = middle - 1 if fine % 2 == 0 else middle + 1
            found = []
            for place, weight in ((middle, 0.75), (other, 0.25)):
                place = max(place, 0) if first else place
                place = min(place, length - 1) if last else place
                found.append((place, weight))
            return found

        for kind in range(9):
            top, bottom = kind // 3 == 0, kind // 3 == 2
            left, right = kind % 3 == 0, kind % 3 == 2
            for a in range(self.wr):
                for b in range(self.wc):
                    at = a * self.width + b
                    for y, wy in terms(a - 2, self.tr, top, bottom):
                        for x, wx in terms(b - 2, self.tc, left, right):
                            if x < 0:
                                side[kind, at, (y + 2) * 2 + x + 2] += wy * wx
                            elif x >= self.tc:
                                side[kind, at, self.cstrip + (y + 2) * 2 + x - self.tc] += wy * wx
                            else:
                                own[kind, at, self.pixel(y, x)] += wy * wx
        return table(own), table(side)

    def pixel(self, y, x):
        base, x = (x // self.pc) * self.span, x % self.pc
        if y < 0:
            return base + x * 2 + y + 2
        if y >= self.tr:
            return base + self.lead + self.pt + x * 2 + y - self.tr
        return base + self.lead + x * self.tr + y

    def row_strips(self):
        pick = np.zeros((2 * self.lead, self.pt), np.float32)
        for x in range(self.pc):
            for y in range(2):
                pick[x * 2 + y, x * self.tr + self.tr - 2 + y] = 1
                pick[self.lead + x * 2 + y, x * self.tr + y] = 1
        return table(pick)

    def coarse_strips(self):
        pick = np.zeros((2 * self.cstrip, 2 * self.span), np.float32)
        for y in range(-2, self.tr + 2):
            for x in range(2):
                pick[(y + 2) * 2 + x, self.pixel(y, x)] = 1
                pick[self.cstrip + (y + 2) * 2 + x, self.pixel(y, self.tc - 2 + x)] = 1
        return table(pick)

    def low_strips(self):
        pick = np.zeros((2 * self.lstrip, self.low), np.float32)
        for y in range(self.wr):
            for x in range(2):
                pick[y * 2 + x, y * self.fc + x] = 1
                pick[self.lstrip + y * 2 + x, y * self.fc + self.fc - 2 + x] = 1
        return table(pick)

    def low_window(self):
        pick = np.zeros((self.window, self.low + 2 * self.lstrip), np.float32)
        for y in range(self.wr):
            for b in range(self.wc):
                x = b - 2
                if x < 0:
                    place = self.low + y * 2 + b
                elif x >= self.fc:
                    place = self.low + self.lstrip + y * 2 + x - self.fc
                else:
                    place = y * self.fc + x
                pick[y * self.width + b, place] = 1
        return table(pick)


def dot(a, b):
    return jnp.dot(a, b, preferred_element_type=F32)


def dot_t(a, b):
    return lax.dot_general(a, b, (((1,), (1,)), ((), ())), preferred_element_type=F32)


def kernel(
    plan,
    feat_ref, low_ref, point_ref, atrous_ref, pool_ref, aspp_bias_ref, proj_ref, proj_bias_ref,
    low_weight_ref, low_bias_ref, conv1_ref, conv1_bias_ref, conv2_ref, conv2_bias_ref,
    up_own_ref, up_side_ref, rpick_ref, cpick_ref, lpick_ref, lwindow_ref,
    out_ref,
    gathered, weights, turned, low_in, proj, conv1, conv2, up_own, up_side, lwindow,
    sums, zsend, zrecv, pools, branch_pool, branches, brecv, proj_blocks,
    cstrips, crecv, low_all, lsend, reduced_window, shifted, low_part, up_window, hidden,
    local_sem, feat_send, feat_recv, z_send, z_recv, pool_send, pool_recv, bp_send, bp_recv,
    b_send, b_recv, c_send, c_recv, lr_send, lr_recv, lc_send, lc_recv,
):
    rows, cols = plan.rows, plan.cols
    tile, tc, width = plan.tile, plan.tc, plan.width
    dp, row, col = lax.axis_index("dp"), lax.axis_index("row"), lax.axis_index("col")
    own, depth = point_ref.shape
    joined = own * rows

    def row_peer(step):
        return lax.rem(row + step, rows)

    def col_peer(step):
        return lax.rem(col + step, cols)

    barrier = pltpu.get_barrier_semaphore()
    for step in range(1, rows):
        pl.semaphore_signal(barrier, inc=1, device_id=(dp, row_peer(step), col), device_id_type=MESH)
    for step in range(1, cols):
        pl.semaphore_signal(barrier, inc=1, device_id=(dp, row, col_peer(step)), device_id_type=MESH)
    pl.semaphore_wait(barrier, rows + cols - 2)

    pt = plan.pt

    def block(owner, begin=0, size=pt):
        return pl.ds(pl.multiple_of(owner * pt + begin, 16), size)

    def send_block(src, owner, half_tile, begin, size, target, at):
        copy = pltpu.make_async_remote_copy(
            src_ref=src, dst_ref=gathered.at[half_tile, block(owner, begin, size)],
            send_sem=feat_send.at[half_tile, at], recv_sem=feat_recv.at[half_tile, at],
            device_id=(dp, target, col), device_id_type=MESH,
        )
        copy.start()
        return copy

    feats = [[], []]
    passing = rows == 4
    if passing:
        beside = row + 1 - 2 * lax.rem(row, 2)
        across = row + 2 - 4 * (row // 2)
    longer = up16(pt // 2)
    ranges = [((0, longer), (longer, pt - longer)), ((0, pt - longer), (pt - longer, longer))]

    def send_features(half_tile):
        made = feats[half_tile]
        if passing:
            ends = [feat_ref.at[pl.ds(half_tile * pt + begin, size)] for begin, size in ranges[half_tile]]
            for number, target, at in ((0, beside, 0), (1, across, 2), (1, beside, 1), (0, across, 3)):
                made.append(send_block(ends[number], row, half_tile, *ranges[half_tile][number], target, at))
        else:
            src = feat_ref.at[pl.ds(half_tile * pt, pt)]
            for step in range(1, rows):
                made.append(send_block(src, row, half_tile, 0, pt, row_peer(step), step - 1))

    def pass_on(half_tile):
        if passing:
            made = feats[half_tile]
            for number, source, target, at in ((0, beside, across, 4), (1, across, beside, 5)):
                made[number].wait_recv()
                begin, size = ranges[half_tile][number]
                src = gathered.at[half_tile, block(source, begin, size)]
                made.append(send_block(src, source, half_tile, begin, size, target, at))

    def wait_features(half_tile):
        copies["feat%d" % half_tile].wait()
        for copy in feats[half_tile][2 if passing else 0:]:
            copy.wait_recv()

    send_features(0)

    copies = {}
    numbered = [
        ("low", low_ref, low_in),
        ("feat0", feat_ref.at[pl.ds(0, pt)], gathered.at[0, block(row)]),
        ("feat1", feat_ref.at[pl.ds(pt, pt)], gathered.at[1, block(row)]),
        ("proj", proj_ref, proj),
        ("conv1", conv1_ref, conv1),
        ("conv2", conv2_ref, conv2),
        ("lwindow", lwindow_ref, lwindow),
    ]
    kind = jnp.where(row == 0, 0, jnp.where(row == rows - 1, 2, 1)) * 3 + jnp.where(
        col == 0, 0, jnp.where(col == cols - 1, 2, 1)
    )
    numbered.append(("up_own", up_own_ref.at[kind], up_own))
    numbered.append(("up_side", up_side_ref.at[kind], up_side))
    for place, (number, tap) in enumerate(plan.taps):
        for slot, j in enumerate((0, 2, 1)):
            numbered.append((
                ("tap", place, slot), atrous_ref.at[number, tap, j],
                weights.at[place, pl.ds(slot * own, own)],
            ))
        if tap == 1 and number < 2:
            numbered.append((
                ("tap", place, 3), (point_ref, pool_ref)[number], weights.at[place, pl.ds(3 * own, own)]
            ))
        else:
            weights[place, pl.ds(3 * own, own), :] = jnp.zeros((own, depth), BF16)
    for place, (name, src, dst) in enumerate(numbered):
        copies[name] = pltpu.make_async_copy(src, dst, local_sem.at[place])
        copies[name].start()

    for half_number in range(2):
        empty = jnp.zeros((plan.lead, 4 * own), BF16)
        branches[half_number, 0, pl.ds(0, plan.lead), :] = empty
        branches[half_number, rows - 1, pl.ds(plan.lead + pt, plan.lead), :] = empty
    distances = [rate // tc for rate in RATES]
    for number, far in enumerate(distances):
        @pl.when(col < far)
        def _():
            for half_tile in range(2):
                zrecv[half_tile, number, 0] = jnp.zeros(zrecv.shape[3:], BF16)

        @pl.when(col + far >= cols)
        def _():
            for half_tile in range(2):
                zrecv[half_tile, number, 1] = jnp.zeros(zrecv.shape[3:], BF16)

    low_ends = (pl.ds(0, plan.lhalo), pl.ds(plan.low - plan.lhalo, plan.lhalo))
    low_sides = (pl.ds(plan.low, plan.lstrip), pl.ds(plan.low + plan.lstrip, plan.lstrip))
    for side, edge in ((0, row == 0), (1, row == rows - 1)):
        @pl.when(edge)
        def _():
            low_all[low_ends[side], :] = jnp.zeros((plan.lhalo, low_all.shape[1]), BF16)

    for side, edge in ((0, col == 0), (1, col == cols - 1)):
        @pl.when(edge)
        def _():
            low_all[low_sides[side], :] = jnp.zeros((plan.lstrip, low_all.shape[1]), BF16)
            crecv[side] = jnp.zeros(crecv.shape[1:], BF16)

    def pair(refs, sends, recvs, along):
        made = []
        for side in range(2):
            src, dst = refs[side]
            step = -1 if side == 0 else 1
            if along == "row":
                there = row + step >= 0 if side == 0 else row + step < rows
                target = (dp, lax.rem(row + step + rows, rows), col)
            else:
                there = col + step >= 0 if side == 0 else col + step < cols
                target = (dp, row, lax.rem(col + step + cols, cols))
            made.append((there, pltpu.make_async_remote_copy(
                src_ref=src, dst_ref=dst, send_sem=sends.at[side], recv_sem=recvs.at[1 - side],
                device_id=target, device_id_type=MESH,
            ), recvs.at[side], refs[1 - side][1]))
        return made

    def start_pair(made):
        for there, copy, _, _ in made:
            @pl.when(there)
            def _():
                copy.start()

    def wait_recv_pair(made):
        for there, copy, sem, landed in made:
            @pl.when(there)
            def _():
                pltpu.make_async_copy(landed, landed, sem).wait()

    def wait_send_pair(made):
        for there, copy, _, _ in made:
            @pl.when(there)
            def _():
                copy.wait_send()

    piece = min(256, depth)

    def turn_weights():
        for name, copy in copies.items():
            if name[0] == "tap":
                copy.wait()
        for place in range(len(plan.taps)):
            for begin in range(0, depth, piece):
                turned[place, pl.ds(begin, piece), :] = weights[place, :, pl.ds(begin, piece)].T

    def products(half_tile, number):
        for place, (which, tap) in enumerate(plan.taps):
            if which == number and tap == 1:
                sums[half_tile, number] = dot(gathered[half_tile], turned[place])
        for place, (which, tap) in enumerate(plan.taps):
            if which == number and tap != 1:
                offset = (tap - 1) * RATES[number]
                whole, rest = offset // plan.tr, offset % plan.tr
                used = [whole, whole + 1] if rest else [whole]
                first = max(0, used[0])
                final = min(rows, rows + used[-1])
                size = (final - first) * pt
                term = dot(gathered[half_tile, pl.ds(first * pt, size), :], turned[place])
                if rest:
                    term = term.reshape(size // plan.tr, plan.tr, 4 * own)
                    term = pltpu.roll(term, plan.tr - rest, 1)
                    upper = lax.broadcasted_iota(jnp.int32, term.shape, 1) < plan.tr - rest
                    terms = [jnp.where(upper, term, 0.0), jnp.where(upper, 0.0, term)]
                    terms = [value.reshape(size, 4 * own) for value in terms]
                else:
                    terms = [term]
                for step, value in zip(used, terms):
                    begin, end = max(0, -step), min(rows, rows - step)
                    count = (end - begin) * pt
                    if count > 0:
                        skip = (begin + step - first) * pt
                        sums[half_tile, number, pl.ds(begin * pt, count), :] += value[skip:skip + count]

    copies["low"].wait()
    reduced = dot_t(low_in[...], low_weight_ref[...]) + low_bias_ref[...]
    low_all[pl.ds(plan.lhalo, plan.fr * plan.fc), :] = jnp.maximum(reduced, 0.0).astype(BF16)
    low_rows = pair(
        (
            (low_all.at[pl.ds(plan.lhalo, plan.lhalo)], low_all.at[low_ends[1]]),
            (low_all.at[pl.ds(plan.low - 2 * plan.lhalo, plan.lhalo)], low_all.at[low_ends[0]]),
        ),
        lr_send, lr_recv, "row",
    )
    start_pair(low_rows)

    half = plan.half
    sideways = [[None] * 3, [None] * 3]
    pool_copies = []

    def spread(half_tile, number):
        for side in range(2):
            lanes = pl.ds(side * own, own)
            zsend[half_tile, number, side] = jnp.concatenate(
                [sums[half_tile, number, pl.ds(part * half, half), lanes] for part in range(2)], axis=1
            ).astype(BF16)
        made = []
        for side, far in ((0, distances[number]), (1, -distances[number])):
            there = col + far < cols if far > 0 else col + far >= 0
            come = col - far < cols if far < 0 else col - far >= 0
            copy = pltpu.make_async_remote_copy(
                src_ref=zsend.at[half_tile, number, side], dst_ref=zrecv.at[half_tile, number, side],
                send_sem=z_send.at[half_tile, number, side], recv_sem=z_recv.at[half_tile, number, side],
                device_id=(dp, row, lax.rem(col + far + 4 * cols, cols)), device_id_type=MESH,
            )
            made.append((there, come, copy))

            @pl.when(there)
            def _():
                copy.start()
        sideways[half_tile][number] = made

    def spread_pool():
        part = sum(
            jnp.sum(sums[half_tile, 1, :, pl.ds(3 * own, own)], axis=0, keepdims=True)
            for half_tile in range(2)
        )
        pools[col] = jnp.broadcast_to(part, (8, own))
        for step in range(1, cols):
            copy = pltpu.make_async_remote_copy(
                src_ref=pools.at[col], dst_ref=pools.at[col],
                send_sem=pool_send.at[step - 1], recv_sem=pool_recv.at[step - 1],
                device_id=(dp, row, col_peer(step)), device_id_type=MESH,
            )
            copy.start()
            pool_copies.append(copy)

    def bias(number):
        return aspp_bias_ref[pl.ds(number, 1), :]

    def point_branch(half_tile, part):
        value = sums[half_tile, 0, pl.ds(part * half, half), pl.ds(3 * own, own)]
        return jnp.maximum(value + bias(0), 0.0).astype(BF16)

    def atrous_branch(half_tile, number, part):
        lanes = pl.ds(part * own, own)
        value = sums[half_tile, number, pl.ds(part * half, half), pl.ds(2 * own, own)]
        for side in range(2):
            value = value + zrecv[half_tile, number, side, :, lanes].astype(F32)
        return jnp.maximum(value + bias(number + 1), 0.0).astype(BF16)

    b_copies = [[], []]

    def send_branches(half_tile):
        for number in (2, 1, 0):
            for there, come, copy in sideways[half_tile][number]:
                @pl.when(come)
                def _():
                    copy.wait_recv()
        joint = []
        for part in range(2):
            made = [point_branch(half_tile, part)]
            made += [atrous_branch(half_tile, number, part) for number in range(3)]
            joint.append(jnp.concatenate(made, axis=1))
        joint = jnp.concatenate(joint, axis=0)
        for place in range(rows):
            value = joint[place * pt:(place + 1) * pt]
            branches[half_tile, place, pl.ds(plan.lead, pt), :] = value
            ends = dot(rpick_ref[:, pl.ds(0, pt)], value).astype(BF16)
            if place + 1 < rows:
                branches[half_tile, place + 1, pl.ds(0, plan.lead), :] = ends[: plan.lead]
            if place > 0:
                branches[half_tile, place - 1, pl.ds(plan.lead + pt, plan.lead), :] = ends[plan.lead:]
        for step in range(1, rows):
            copy = pltpu.make_async_remote_copy(
                src_ref=branches.at[half_tile, row_peer(step)], dst_ref=brecv.at[half_tile, row],
                send_sem=b_send.at[half_tile, step - 1], recv_sem=b_recv.at[half_tile, step - 1],
                device_id=(dp, row_peer(step), col), device_id_type=MESH,
            )
            copy.start()
            b_copies[half_tile].append(copy)
        brecv[half_tile, row] = branches[half_tile, row]

    pass_on(0)
    send_features(1)
    turn_weights()
    wait_features(0)
    for number in (2, 1, 0):
        products(0, number)
        spread(0, number)
    pass_on(1)
    wait_recv_pair(low_rows)
    lsend[...] = dot(lpick_ref[:, pl.ds(0, plan.low)], low_all[pl.ds(0, plan.low), :]).astype(BF16)
    low_cols = pair(
        (
            (lsend.at[pl.ds(0, plan.lstrip)], low_all.at[low_sides[1]]),
            (lsend.at[pl.ds(plan.lstrip, plan.lstrip)], low_all.at[low_sides[0]]),
        ),
        lc_send, lc_recv, "col",
    )
    start_pair(low_cols)

    copies["proj"].wait()
    for w in range(rows):
        for branch in range(4):
            proj_blocks[w, pl.ds(branch * own, own), :] = proj[
                pl.ds(branch * joined + w * own, own), :
            ]

    wait_recv_pair(low_cols)
    copies["lwindow"].wait()
    copies["conv1"].wait()
    reduced_window[...] = dot(lwindow[:, pl.ds(0, low_all.shape[0])], low_all[...]).astype(BF16)
    wide = conv1.shape[3]
    fine = conv1.shape[2] - low_all.shape[1]
    hidden_px = (plan.wr - 2) * width
    out_px = plan.fr * width
    tail = jnp.zeros((8, wide), F32)
    for j in range(2):
        shifted[j, pl.ds(hidden_px, 8), :] = tail
    for j in range(3):
        total = None
        for i in range(3):
            term = dot(
                reduced_window[pl.ds(i * width, hidden_px), :],
                conv1[i, j, pl.ds(fine, low_all.shape[1]), :],
            )
            total = term if total is None else total + term
        if j == 0:
            low_part[...] = total + conv1_bias_ref[...]
        else:
            shifted[j - 1, pl.ds(0, hidden_px), :] = total
    low_part[...] += shifted[0, pl.ds(1, hidden_px), :] + shifted[1, pl.ds(2, hidden_px), :]

    send_branches(0)
    wait_features(1)
    for number in (2, 1, 0):
        products(1, number)
        spread(1, number)
        if number == 1:
            spread_pool()

    for copy in pool_copies:
        copy.wait_recv()
    pooled = pools[0]
    for place in range(1, cols):
        pooled = pooled + pools[place]
    pooled = pooled / (plan.height * cols * tc)
    last = jnp.maximum(pooled + aspp_bias_ref[pl.ds(4, 1), :], 0.0)
    branch_pool[row] = jnp.concatenate([last, last], axis=0).astype(BF16)
    bp_copies = []
    for step in range(1, rows):
        copy = pltpu.make_async_remote_copy(
            src_ref=branch_pool.at[row], dst_ref=branch_pool.at[row],
            send_sem=bp_send.at[step - 1], recv_sem=bp_recv.at[step - 1],
            device_id=(dp, row_peer(step), col), device_id_type=MESH,
        )
        copy.start()
        bp_copies.append(copy)

    send_branches(1)
    for copy in bp_copies:
        copy.wait_recv()
    constant = proj_bias_ref[...]
    for w in range(rows):
        constant = constant + dot(
            branch_pool[w], proj[pl.ds(4 * joined + w * own, own), :]
        )[0:1, :]
    coarse = []
    for half_tile in range(2):
        for copy in b_copies[half_tile]:
            copy.wait_recv()
        total = constant
        for w in range(rows):
            total = total + dot(brecv[half_tile, w], proj_blocks[w])
        coarse.append(total)
    coarse = jnp.concatenate(coarse, axis=0)
    coarse = jnp.maximum(coarse, 0.0).astype(BF16)

    cstrips[...] = dot(cpick_ref[:, pl.ds(0, 2 * plan.span)], coarse).astype(BF16)
    coarse_cols = pair(
        (
            (cstrips.at[pl.ds(0, plan.cstrip)], crecv.at[1]),
            (cstrips.at[pl.ds(plan.cstrip, plan.cstrip)], crecv.at[0]),
        ),
        c_send, c_recv, "col",
    )
    start_pair(coarse_cols)
    copies["up_own"].wait()
    copies["up_side"].wait()
    copies["conv2"].wait()
    up_sums = dot(up_own[:, pl.ds(0, 2 * plan.span)], coarse)
    wait_recv_pair(coarse_cols)
    strips = jnp.concatenate([crecv[0], crecv[1]], axis=0)
    up_window[...] = (up_sums + dot(up_side[:, pl.ds(0, 2 * plan.cstrip)], strips)).astype(BF16)

    def convolve(source, weight, depth, size):
        wide_in = jnp.concatenate(
            [source[pl.ds(i * width, size), :] for i in range(3)], axis=1
        )
        first = None
        for j in range(3):
            stacked = jnp.concatenate(
                [weight[i, j, pl.ds(0, depth), :] for i in range(3)], axis=0
            )
            total = dot(wide_in, stacked)
            if j == 0:
                first = total
            else:
                shifted[j - 1, pl.ds(0, size), :] = total
        return first + shifted[0, pl.ds(1, size), :] + shifted[1, pl.ds(2, size), :]

    result = convolve(up_window, conv1, fine, hidden_px) + low_part[...]
    result = jnp.maximum(result, 0.0).reshape(plan.wr - 2, width, wide)
    a = lax.broadcasted_iota(jnp.int32, result.shape, 0)
    b = lax.broadcasted_iota(jnp.int32, result.shape, 1)
    low_a = jnp.where(row == 0, 1, 0)
    high_a = jnp.where(row == rows - 1, plan.fr + 1, plan.fr + 2)
    low_b = jnp.where(col == 0, 1, 0)
    high_b = jnp.where(col == cols - 1, plan.fc + 1, plan.fc + 2)
    inside = (a >= low_a) & (a < high_a) & (b >= low_b) & (b < high_b)
    result = jnp.where(inside, result, 0.0)
    hidden[...] = result.reshape(hidden_px, wide).astype(BF16)

    result = convolve(hidden, conv2, conv2.shape[2], out_px) + conv2_bias_ref[...]
    result = jnp.maximum(result, 0.0).reshape(plan.fr, width, wide)
    out_ref[...] = result[:, : plan.fc, :].astype(BF16)

    for copy in feats[0] + feats[1] + pool_copies + bp_copies + b_copies[0] + b_copies[1]:
        copy.wait_send()
    for made in sideways[0] + sideways[1]:
        for there, come, copy in made:
            @pl.when(there)
            def _():
                copy.wait_send()
    for made in (low_rows, low_cols, coarse_cols):
        wait_send_pair(made)


def on_device(
    plan,
    features, low_level, point_weight, atrous_weight, pool_weight, aspp_bias, proj_weight, proj_bias,
    low_weight, low_bias, conv1_weight, conv1_bias, conv2_weight, conv2_bias,
):
    own, depth = point_weight.shape[::-1]
    out_width = proj_weight.shape[1]
    red = low_weight.shape[1]
    rows, cols = plan.rows, plan.cols
    taps = len(plan.taps)
    wide = conv1_weight.shape[3]
    up_own, up_side = plan.upsample()
    any_spec = pl.BlockSpec(memory_space=pl.ANY)
    vmem = pl.BlockSpec(memory_space=pltpu.VMEM)
    dma = pltpu.SemaphoreType.DMA
    hidden_px = (plan.wr - 2) * plan.width
    feat_sends = 6 if rows == 4 else rows - 1
    scratch = [
        pltpu.VMEM((2, plan.pixels, depth), BF16),
        pltpu.VMEM((taps, 4 * own, depth), BF16),
        pltpu.VMEM((taps, depth, 4 * own), BF16),
        pltpu.VMEM((plan.fr * plan.fc, low_level.shape[2]), BF16),
        pltpu.VMEM(proj_weight.shape, BF16),
        pltpu.VMEM(conv1_weight.shape, BF16),
        pltpu.VMEM(conv2_weight.shape, BF16),
        pltpu.VMEM(up_own.shape[1:], BF16),
        pltpu.VMEM(up_side.shape[1:], BF16),
        pltpu.VMEM(plan.low_window().shape, BF16),
        pltpu.VMEM((2, 3, plan.pixels, 4 * own), F32),
        pltpu.VMEM((2, 3, 2, plan.half, 2 * own), BF16),
        pltpu.VMEM((2, 3, 2, plan.half, 2 * own), BF16),
        pltpu.VMEM((cols, 8, own), F32),
        pltpu.VMEM((rows, 16, own), BF16),
        pltpu.VMEM((2, rows, plan.span, 4 * own), BF16),
        pltpu.VMEM((2, rows, plan.span, 4 * own), BF16),
        pltpu.VMEM((rows, 4 * own, out_width), BF16),
        pltpu.VMEM((2 * plan.cstrip, out_width), BF16),
        pltpu.VMEM((2, plan.cstrip, out_width), BF16),
        pltpu.VMEM((plan.low + 2 * plan.lstrip, red), BF16),
        pltpu.VMEM((2 * plan.lstrip, red), BF16),
        pltpu.VMEM((plan.window, red), BF16),
        pltpu.VMEM((2, hidden_px + 8, wide), F32),
        pltpu.VMEM((hidden_px, wide), F32),
        pltpu.VMEM((plan.window, out_width), BF16),
        pltpu.VMEM((hidden_px, wide), BF16),
        dma((9 + 4 * taps,)),
        dma((2, feat_sends)), dma((2, feat_sends)),
        dma((2, 3, 2)), dma((2, 3, 2)),
        dma((cols - 1,)), dma((cols - 1,)),
        dma((rows - 1,)), dma((rows - 1,)),
        dma((2, rows - 1)), dma((2, rows - 1)),
        dma((2,)), dma((2,)), dma((2,)), dma((2,)), dma((2,)), dma((2,)),
    ]
    return pl.pallas_call(
        functools.partial(kernel, plan),
        out_shape=jax.ShapeDtypeStruct((plan.fr, plan.fc, wide), BF16),
        in_specs=[
            any_spec, any_spec, any_spec, any_spec, any_spec, vmem, any_spec, vmem,
            vmem, vmem, any_spec, vmem, any_spec, vmem,
            any_spec, any_spec, vmem, vmem, vmem, any_spec,
        ],
        out_specs=vmem,
        scratch_shapes=scratch,
        compiler_params=pltpu.CompilerParams(
            collective_id=0, has_side_effects=True, vmem_limit_bytes=60 * 1024 * 1024
        ),
    )(
        jnp.transpose(features, (1, 0, 2)).reshape(plan.tile, depth),
        low_level.reshape(plan.fr * plan.fc, low_level.shape[2]),
        point_weight.T, jnp.swapaxes(atrous_weight, 3, 4), pool_weight.T, aspp_bias, proj_weight,
        proj_bias[None], low_weight.T, low_bias[None], conv1_weight, conv1_bias[None], conv2_weight, conv2_bias[None],
        jnp.asarray(up_own, BF16), jnp.asarray(up_side, BF16),
        jnp.asarray(plan.row_strips(), BF16), jnp.asarray(plan.coarse_strips(), BF16), jnp.asarray(plan.low_strips(), BF16),
        jnp.asarray(plan.low_window(), BF16),
    )


def solution(mesh):
    placed = (
        P(("dp", "row"), "col", None),
        P(("dp", "row"), "col", None),
        P(None, "row"),
        P(None, None, None, None, "row"),
        P(None, "row"),
        P(None, "row"),
        P(),
        P(),
        P(),
        P(),
        P(),
        P(),
        P(),
        P(),
    )

    def local(features, *others):
        plan = Plan(mesh.shape["row"], mesh.shape["col"], features.shape[0], features.shape[1])
        return on_device(plan, features, *others)

    return jax.shard_map(
        local,
        mesh=mesh,
        in_specs=placed,
        out_specs=P(("dp", "row"), "col", None),
        check_vma=False,
    )
```

```python
import functools

import jax
import jax.numpy as jnp
import numpy as np
from jax import lax
from jax.experimental import pallas as pl
from jax.experimental.pallas import tpu as pltpu
from jax.sharding import PartitionSpec as P

RATES = (12, 24, 36)
MESH = pl.DeviceIdType.MESH
F32 = jnp.float32
BF16 = jnp.bfloat16


def up16(value):
    return -(-value // 16) * 16


def table(values):
    lanes = -values.shape[-1] % 128
    return np.pad(values, [(0, 0)] * (values.ndim - 1) + [(0, lanes)])


class Plan:
    def __init__(self, rows, cols, tile_rows, tile_cols):
        self.rows, self.cols = rows, cols
        self.tr, self.tc = tile_rows, tile_cols
        self.tile = tile_rows * tile_cols
        self.height = rows * tile_rows
        self.pixels = self.height * tile_cols
        self.half = self.pixels // 2
        self.lead = up16(2 * tile_cols)
        self.span = self.tile + 2 * self.lead
        self.cstrip = up16((tile_rows + 4) * 2)
        self.fr, self.fc = 2 * tile_rows, 2 * tile_cols
        self.wr, self.wc = self.fr + 4, self.fc + 4
        self.width = 32 * (-(-self.wc // 32))
        self.window = self.wr * self.width
        self.lhalo = 2 * self.fc
        self.low = self.wr * self.fc
        self.lstrip = up16(self.wr * 2)
        self.taps = []
        for number, rate in enumerate(RATES):
            for tap in range(3):
                if abs(tap - 1) * rate < self.height:
                    self.taps.append((number, tap))

    def upsample(self):
        own = np.zeros((9, self.window, self.span), np.float32)
        side = np.zeros((9, self.window, 2 * self.cstrip), np.float32)

        def terms(fine, length, first, last):
            if (first and fine < 0) or (last and fine >= 2 * length):
                return []
            middle = fine // 2
            other = middle - 1 if fine % 2 == 0 else middle + 1
            found = []
            for place, weight in ((middle, 0.75), (other, 0.25)):
                place = max(place, 0) if first else place
                place = min(place, length - 1) if last else place
                found.append((place, weight))
            return found

        for kind in range(9):
            top, bottom = kind // 3 == 0, kind // 3 == 2
            left, right = kind % 3 == 0, kind % 3 == 2
            for a in range(self.wr):
                for b in range(self.wc):
                    at = a * self.width + b
                    for y, wy in terms(a - 2, self.tr, top, bottom):
                        for x, wx in terms(b - 2, self.tc, left, right):
                            if x < 0:
                                side[kind, at, (y + 2) * 2 + x + 2] += wy * wx
                            elif x >= self.tc:
                                side[kind, at, self.cstrip + (y + 2) * 2 + x - self.tc] += wy * wx
                            else:
                                own[kind, at, self.pixel(y, x)] += wy * wx
        return table(own), table(side)

    def pixel(self, y, x):
        if y < 0:
            return x * 2 + y + 2
        if y >= self.tr:
            return self.lead + self.tile + x * 2 + y - self.tr
        return self.lead + x * self.tr + y

    def row_strips(self):
        pick = np.zeros((2 * self.lead, self.tile), np.float32)
        for x in range(self.tc):
            for y in range(2):
                pick[x * 2 + y, x * self.tr + self.tr - 2 + y] = 1
                pick[self.lead + x * 2 + y, x * self.tr + y] = 1
        return table(pick)

    def coarse_strips(self):
        pick = np.zeros((2 * self.cstrip, self.span), np.float32)
        for y in range(-2, self.tr + 2):
            for x in range(2):
                pick[(y + 2) * 2 + x, self.pixel(y, x)] = 1
                pick[self.cstrip + (y + 2) * 2 + x, self.pixel(y, self.tc - 2 + x)] = 1
        return table(pick)

    def low_strips(self):
        pick = np.zeros((2 * self.lstrip, self.low), np.float32)
        for y in range(self.wr):
            for x in range(2):
                pick[y * 2 + x, y * self.fc + x] = 1
                pick[self.lstrip + y * 2 + x, y * self.fc + self.fc - 2 + x] = 1
        return table(pick)

    def low_window(self):
        pick = np.zeros((self.window, self.low + 2 * self.lstrip), np.float32)
        for y in range(self.wr):
            for b in range(self.wc):
                x = b - 2
                if x < 0:
                    place = self.low + y * 2 + b
                elif x >= self.fc:
                    place = self.low + self.lstrip + y * 2 + x - self.fc
                else:
                    place = y * self.fc + x
                pick[y * self.width + b, place] = 1
        return table(pick)


def dot(a, b):
    return jnp.dot(a, b, preferred_element_type=F32)


def dot_t(a, b):
    return lax.dot_general(a, b, (((1,), (1,)), ((), ())), preferred_element_type=F32)


def kernel(
    plan,
    feat_ref, low_ref, point_ref, atrous_ref, pool_ref, aspp_bias_ref, proj_ref, proj_bias_ref,
    low_weight_ref, low_bias_ref, conv1_ref, conv1_bias_ref, conv2_ref, conv2_bias_ref,
    up_own_ref, up_side_ref, rpick_ref, cpick_ref, lpick_ref, lwindow_ref,
    out_ref,
    gathered, weights, turned, low_in, proj, conv1, conv2, up_own, up_side, lwindow,
    sums, zsend, zrecv, pools, branch_pool, branches, brecv, proj_blocks,
    cstrips, crecv, low_all, lsend, reduced_window, shifted, low_part, up_window, hidden,
    local_sem, feat_send, feat_recv, z_send, z_recv, pool_send, pool_recv, bp_send, bp_recv,
    b_send, b_recv, c_send, c_recv, lr_send, lr_recv, lc_send, lc_recv,
):
    rows, cols = plan.rows, plan.cols
    tile, tc, width = plan.tile, plan.tc, plan.width
    dp, row, col = lax.axis_index("dp"), lax.axis_index("row"), lax.axis_index("col")
    own, depth = point_ref.shape
    joined = own * rows

    def row_peer(step):
        return lax.rem(row + step, rows)

    def col_peer(step):
        return lax.rem(col + step, cols)

    barrier = pltpu.get_barrier_semaphore()
    for step in range(1, rows):
        pl.semaphore_signal(barrier, inc=1, device_id=(dp, row_peer(step), col), device_id_type=MESH)
    for step in range(1, cols):
        pl.semaphore_signal(barrier, inc=1, device_id=(dp, row, col_peer(step)), device_id_type=MESH)
    pl.semaphore_wait(barrier, rows + cols - 2)

    def block(owner, part=0, parts=1):
        size = tile // parts
        return pl.ds(pl.multiple_of(owner * tile + part * size, 16), size)

    def send_block(src, owner, part, parts, target, at):
        copy = pltpu.make_async_remote_copy(
            src_ref=src, dst_ref=gathered.at[block(owner, part, parts)],
            send_sem=feat_send.at[at], recv_sem=feat_recv.at[at],
            device_id=(dp, target, col), device_id_type=MESH,
        )
        copy.start()
        return copy

    feats = []
    passing = rows == 4
    if passing:
        beside = row + 1 - 2 * lax.rem(row, 2)
        across = row + 2 - 4 * (row // 2)
        size = tile // 2
        ends = [feat_ref.at[pl.ds(part * size, size)] for part in range(2)]
        feats.append(send_block(ends[0], row, 0, 2, beside, 0))
        feats.append(send_block(ends[1], row, 1, 2, across, 2))
        feats.append(send_block(ends[1], row, 1, 2, beside, 1))
        feats.append(send_block(ends[0], row, 0, 2, across, 3))
    else:
        for step in range(1, rows):
            feats.append(send_block(feat_ref, row, 0, 1, row_peer(step), step - 1))

    copies = {}
    numbered = [
        ("low", low_ref, low_in),
        ("feat", feat_ref, gathered.at[pl.ds(pl.multiple_of(row * tile, 16), tile)]),
        ("proj", proj_ref, proj),
        ("conv1", conv1_ref, conv1),
        ("conv2", conv2_ref, conv2),
        ("lwindow", lwindow_ref, lwindow),
    ]
    kind = jnp.where(row == 0, 0, jnp.where(row == rows - 1, 2, 1)) * 3 + jnp.where(
        col == 0, 0, jnp.where(col == cols - 1, 2, 1)
    )
    numbered.append(("up_own", up_own_ref.at[kind], up_own))
    numbered.append(("up_side", up_side_ref.at[kind], up_side))
    for place, (number, tap) in enumerate(plan.taps):
        for slot, j in enumerate((0, 2, 1)):
            numbered.append((
                ("tap", place, slot), atrous_ref.at[number, tap, j],
                weights.at[place, pl.ds(slot * own, own)],
            ))
        if tap == 1 and number < 2:
            numbered.append((
                ("tap", place, 3), (point_ref, pool_ref)[number], weights.at[place, pl.ds(3 * own, own)]
            ))
        else:
            weights[place, pl.ds(3 * own, own), :] = jnp.zeros((own, depth), BF16)
    for place, (name, src, dst) in enumerate(numbered):
        copies[name] = pltpu.make_async_copy(src, dst, local_sem.at[place])
        copies[name].start()

    def pass_on():
        if passing:
            feats[0].wait_recv()
            feats.append(send_block(gathered.at[block(beside, 0, 2)], beside, 0, 2, across, 4))
            feats[1].wait_recv()
            feats.append(send_block(gathered.at[block(across, 1, 2)], across, 1, 2, beside, 5))

    for half_number in range(2):
        empty = jnp.zeros((plan.lead, 2 * own), BF16)
        branches[half_number, 0, pl.ds(0, plan.lead), :] = empty
        branches[half_number, rows - 1, pl.ds(plan.lead + tile, plan.lead), :] = empty
    distances = [rate // tc for rate in RATES]
    for number, far in enumerate(distances):
        @pl.when(col < far)
        def _():
            zrecv[number, 0] = jnp.zeros(zrecv.shape[2:], BF16)

        @pl.when(col + far >= cols)
        def _():
            zrecv[number, 1] = jnp.zeros(zrecv.shape[2:], BF16)

    low_ends = (pl.ds(0, plan.lhalo), pl.ds(plan.low - plan.lhalo, plan.lhalo))
    low_sides = (pl.ds(plan.low, plan.lstrip), pl.ds(plan.low + plan.lstrip, plan.lstrip))
    for side, edge in ((0, row == 0), (1, row == rows - 1)):
        @pl.when(edge)
        def _():
            low_all[low_ends[side], :] = jnp.zeros((plan.lhalo, low_all.shape[1]), BF16)

    for side, edge in ((0, col == 0), (1, col == cols - 1)):
        @pl.when(edge)
        def _():
            low_all[low_sides[side], :] = jnp.zeros((plan.lstrip, low_all.shape[1]), BF16)
            crecv[side] = jnp.zeros(crecv.shape[1:], BF16)

    def pair(refs, sends, recvs, along):
        made = []
        for side in range(2):
            src, dst = refs[side]
            step = -1 if side == 0 else 1
            if along == "row":
                there = row + step >= 0 if side == 0 else row + step < rows
                target = (dp, lax.rem(row + step + rows, rows), col)
            else:
                there = col + step >= 0 if side == 0 else col + step < cols
                target = (dp, row, lax.rem(col + step + cols, cols))
            made.append((there, pltpu.make_async_remote_copy(
                src_ref=src, dst_ref=dst, send_sem=sends.at[side], recv_sem=recvs.at[1 - side],
                device_id=target, device_id_type=MESH,
            ), recvs.at[side], refs[1 - side][1]))
        return made

    def start_pair(made):
        for there, copy, _, _ in made:
            @pl.when(there)
            def _():
                copy.start()

    def wait_recv_pair(made):
        for there, copy, sem, landed in made:
            @pl.when(there)
            def _():
                pltpu.make_async_copy(landed, landed, sem).wait()

    def wait_send_pair(made):
        for there, copy, _, _ in made:
            @pl.when(there)
            def _():
                copy.wait_send()

    piece = min(256, depth)

    def turn_weights(places):
        for place in places:
            for name, copy in copies.items():
                if name[:2] == ("tap", place):
                    copy.wait()
            for begin in range(0, depth, piece):
                turned[place, pl.ds(begin, piece), :] = weights[place, :, pl.ds(begin, piece)].T

    def products(number):
        for place, (which, tap) in enumerate(plan.taps):
            if which == number and tap == 1:
                sums[number] = dot(gathered[...], turned[place])
        for place, (which, tap) in enumerate(plan.taps):
            if which == number and tap != 1:
                offset = (tap - 1) * RATES[number]
                whole, rest = offset // plan.tr, offset % plan.tr
                used = [whole, whole + 1] if rest else [whole]
                first = max(0, used[0])
                final = min(rows, rows + used[-1])
                size = (final - first) * tile
                term = dot(gathered[pl.ds(first * tile, size), :], turned[place])
                if rest:
                    term = term.reshape(size // plan.tr, plan.tr, 4 * own)
                    term = pltpu.roll(term, plan.tr - rest, 1)
                    upper = lax.broadcasted_iota(jnp.int32, term.shape, 1) < plan.tr - rest
                    terms = [jnp.where(upper, term, 0.0), jnp.where(upper, 0.0, term)]
                    terms = [value.reshape(size, 4 * own) for value in terms]
                else:
                    terms = [term]
                for step, value in zip(used, terms):
                    begin, end = max(0, -step), min(rows, rows - step)
                    count = (end - begin) * tile
                    if count > 0:
                        skip = (begin + step - first) * tile
                        sums[number, pl.ds(begin * tile, count), :] += value[skip:skip + count]

    copies["low"].wait()
    reduced = dot_t(low_in[...], low_weight_ref[...]) + low_bias_ref[...]
    low_all[pl.ds(plan.lhalo, plan.fr * plan.fc), :] = jnp.maximum(reduced, 0.0).astype(BF16)
    low_rows = pair(
        (
            (low_all.at[pl.ds(plan.lhalo, plan.lhalo)], low_all.at[low_ends[1]]),
            (low_all.at[pl.ds(plan.low - 2 * plan.lhalo, plan.lhalo)], low_all.at[low_ends[0]]),
        ),
        lr_send, lr_recv, "row",
    )
    start_pair(low_rows)

    middle = len(plan.taps) // 2
    turn_weights(range(middle))
    pass_on()
    turn_weights(range(middle, len(plan.taps)))
    wait_recv_pair(low_rows)
    lsend[...] = dot(lpick_ref[:, pl.ds(0, plan.low)], low_all[pl.ds(0, plan.low), :]).astype(BF16)
    low_cols = pair(
        (
            (lsend.at[pl.ds(0, plan.lstrip)], low_all.at[low_sides[1]]),
            (lsend.at[pl.ds(plan.lstrip, plan.lstrip)], low_all.at[low_sides[0]]),
        ),
        lc_send, lc_recv, "col",
    )
    start_pair(low_cols)

    copies["proj"].wait()
    for w in range(rows):
        for slot, branch in enumerate((0, 3, 1, 2)):
            proj_blocks[w, pl.ds(slot * own, own), :] = proj[
                pl.ds(branch * joined + w * own, own), :
            ]

    copies["feat"].wait()
    for copy in feats[2 if passing else 0:]:
        copy.wait_recv()

    half = plan.half
    sideways = [None, None, None]
    pool_copies = []
    for number in (2, 1, 0):
        rate = RATES[number]
        products(number)
        for side in range(2):
            lanes = pl.ds(side * own, own)
            zsend[number, side] = jnp.concatenate(
                [sums[number, pl.ds(0, half), lanes], sums[number, pl.ds(half, half), lanes]], axis=1
            ).astype(BF16)
        made = []
        for side, far in ((0, distances[number]), (1, -distances[number])):
            there = col + far < cols if far > 0 else col + far >= 0
            come = col - far < cols if far < 0 else col - far >= 0
            copy = pltpu.make_async_remote_copy(
                src_ref=zsend.at[number, side], dst_ref=zrecv.at[number, side],
                send_sem=z_send.at[number, side], recv_sem=z_recv.at[number, side],
                device_id=(dp, row, lax.rem(col + far + 4 * cols, cols)), device_id_type=MESH,
            )
            made.append((there, come, copy))

            @pl.when(there)
            def _():
                copy.start()
        sideways[number] = made
        if number == 1:
            part = jnp.sum(sums[number, :, pl.ds(3 * own, own)], axis=0, keepdims=True)
            pools[col] = jnp.broadcast_to(part, (8, own))
            for step in range(1, cols):
                copy = pltpu.make_async_remote_copy(
                    src_ref=pools.at[col], dst_ref=pools.at[col],
                    send_sem=pool_send.at[step - 1], recv_sem=pool_recv.at[step - 1],
                    device_id=(dp, row, col_peer(step)), device_id_type=MESH,
                )
                copy.start()
                pool_copies.append(copy)

    def bias(number):
        return aspp_bias_ref[pl.ds(number, 1), :]

    def point_branch(part):
        value = sums[0, pl.ds(part * half, half), pl.ds(3 * own, own)]
        return jnp.maximum(value + bias(0), 0.0).astype(BF16)

    def arrive(number):
        for there, come, copy in sideways[number]:
            @pl.when(come)
            def _():
                copy.wait_recv()

    def atrous_branch(number, part):
        lanes = pl.ds(part * own, own)
        value = sums[number, pl.ds(part * half, half), pl.ds(2 * own, own)]
        value = value + zrecv[number, 0, :, lanes].astype(F32) + zrecv[number, 1, :, lanes].astype(F32)
        return jnp.maximum(value + bias(number + 1), 0.0).astype(BF16)

    b_copies = [[], []]

    def send_branches(message, made):
        joint = [jnp.concatenate(made(part), axis=1) for part in range(2)]
        joint = jnp.concatenate(joint, axis=0)
        for place in range(rows):
            value = joint[place * tile:(place + 1) * tile]
            branches[message, place, pl.ds(plan.lead, tile), :] = value
            ends = dot(rpick_ref[:, pl.ds(0, tile)], value).astype(BF16)
            if place + 1 < rows:
                branches[message, place + 1, pl.ds(0, plan.lead), :] = ends[: plan.lead]
            if place > 0:
                branches[message, place - 1, pl.ds(plan.lead + tile, plan.lead), :] = ends[plan.lead:]
        for step in range(1, rows):
            copy = pltpu.make_async_remote_copy(
                src_ref=branches.at[message, row_peer(step)], dst_ref=brecv.at[message, row],
                send_sem=b_send.at[message, step - 1], recv_sem=b_recv.at[message, step - 1],
                device_id=(dp, row_peer(step), col), device_id_type=MESH,
            )
            copy.start()
            b_copies[message].append(copy)
        brecv[message, row] = branches[message, row]

    arrive(2)
    send_branches(0, lambda part: [point_branch(part), atrous_branch(2, part)])

    for copy in pool_copies:
        copy.wait_recv()
    pooled = pools[0]
    for place in range(1, cols):
        pooled = pooled + pools[place]
    pooled = pooled / (plan.height * cols * tc)
    last = jnp.maximum(pooled + aspp_bias_ref[pl.ds(4, 1), :], 0.0)
    branch_pool[row] = jnp.concatenate([last, last], axis=0).astype(BF16)
    bp_copies = []
    for step in range(1, rows):
        copy = pltpu.make_async_remote_copy(
            src_ref=branch_pool.at[row], dst_ref=branch_pool.at[row],
            send_sem=bp_send.at[step - 1], recv_sem=bp_recv.at[step - 1],
            device_id=(dp, row_peer(step), col), device_id_type=MESH,
        )
        copy.start()
        bp_copies.append(copy)

    wait_recv_pair(low_cols)
    copies["lwindow"].wait()
    copies["conv1"].wait()
    reduced_window[...] = dot(lwindow[:, pl.ds(0, low_all.shape[0])], low_all[...]).astype(BF16)
    wide = conv1.shape[3]
    fine = conv1.shape[2] - low_all.shape[1]
    hidden_px = (plan.wr - 2) * width
    out_px = plan.fr * width
    tail = jnp.zeros((8, wide), F32)
    for j in range(2):
        shifted[j, pl.ds(hidden_px, 8), :] = tail
    for j in range(3):
        total = None
        for i in range(3):
            term = dot(
                reduced_window[pl.ds(i * width, hidden_px), :],
                conv1[i, j, pl.ds(fine, low_all.shape[1]), :],
            )
            total = term if total is None else total + term
        if j == 0:
            low_part[...] = total + conv1_bias_ref[...]
        else:
            shifted[j - 1, pl.ds(0, hidden_px), :] = total
    low_part[...] += shifted[0, pl.ds(1, hidden_px), :] + shifted[1, pl.ds(2, hidden_px), :]

    arrive(1)
    arrive(0)
    send_branches(1, lambda part: [atrous_branch(0, part), atrous_branch(1, part)])

    for copy in bp_copies:
        copy.wait_recv()
    constant = proj_bias_ref[...]
    for w in range(rows):
        constant = constant + dot(
            branch_pool[w], proj[pl.ds(4 * joined + w * own, own), :]
        )[0:1, :]
    coarse = constant
    for message in range(2):
        for copy in b_copies[message]:
            copy.wait_recv()
        for w in range(rows):
            coarse = coarse + dot(
                brecv[message, w], proj_blocks[w, pl.ds(message * 2 * own, 2 * own), :]
            )
    coarse = jnp.maximum(coarse, 0.0).astype(BF16)

    cstrips[...] = dot(cpick_ref[:, pl.ds(0, plan.span)], coarse).astype(BF16)
    coarse_cols = pair(
        (
            (cstrips.at[pl.ds(0, plan.cstrip)], crecv.at[1]),
            (cstrips.at[pl.ds(plan.cstrip, plan.cstrip)], crecv.at[0]),
        ),
        c_send, c_recv, "col",
    )
    start_pair(coarse_cols)
    copies["up_own"].wait()
    copies["up_side"].wait()
    copies["conv2"].wait()
    up_sums = dot(up_own[:, pl.ds(0, plan.span)], coarse)
    wait_recv_pair(coarse_cols)
    strips = jnp.concatenate([crecv[0], crecv[1]], axis=0)
    up_window[...] = (up_sums + dot(up_side[:, pl.ds(0, 2 * plan.cstrip)], strips)).astype(BF16)

    def convolve(source, weight, depth, size):
        wide_in = jnp.concatenate(
            [source[pl.ds(i * width, size), :] for i in range(3)], axis=1
        )
        first = None
        for j in range(3):
            stacked = jnp.concatenate(
                [weight[i, j, pl.ds(0, depth), :] for i in range(3)], axis=0
            )
            total = dot(wide_in, stacked)
            if j == 0:
                first = total
            else:
                shifted[j - 1, pl.ds(0, size), :] = total
        return first + shifted[0, pl.ds(1, size), :] + shifted[1, pl.ds(2, size), :]

    result = convolve(up_window, conv1, fine, hidden_px) + low_part[...]
    result = jnp.maximum(result, 0.0).reshape(plan.wr - 2, width, wide)
    a = lax.broadcasted_iota(jnp.int32, result.shape, 0)
    b = lax.broadcasted_iota(jnp.int32, result.shape, 1)
    low_a = jnp.where(row == 0, 1, 0)
    high_a = jnp.where(row == rows - 1, plan.fr + 1, plan.fr + 2)
    low_b = jnp.where(col == 0, 1, 0)
    high_b = jnp.where(col == cols - 1, plan.fc + 1, plan.fc + 2)
    inside = (a >= low_a) & (a < high_a) & (b >= low_b) & (b < high_b)
    result = jnp.where(inside, result, 0.0)
    hidden[...] = result.reshape(hidden_px, wide).astype(BF16)

    result = convolve(hidden, conv2, conv2.shape[2], out_px) + conv2_bias_ref[...]
    result = jnp.maximum(result, 0.0).reshape(plan.fr, width, wide)
    out_ref[...] = result[:, : plan.fc, :].astype(BF16)

    for copy in feats + pool_copies + bp_copies + b_copies[0] + b_copies[1]:
        copy.wait_send()
    for made in sideways:
        for there, come, copy in made:
            @pl.when(there)
            def _():
                copy.wait_send()
    for made in (low_rows, low_cols, coarse_cols):
        wait_send_pair(made)


def on_device(
    plan,
    features, low_level, point_weight, atrous_weight, pool_weight, aspp_bias, proj_weight, proj_bias,
    low_weight, low_bias, conv1_weight, conv1_bias, conv2_weight, conv2_bias,
):
    own, depth = point_weight.shape[::-1]
    out_width = proj_weight.shape[1]
    red = low_weight.shape[1]
    rows, cols = plan.rows, plan.cols
    taps = len(plan.taps)
    wide = conv1_weight.shape[3]
    up_own, up_side = plan.upsample()
    any_spec = pl.BlockSpec(memory_space=pl.ANY)
    vmem = pl.BlockSpec(memory_space=pltpu.VMEM)
    dma = pltpu.SemaphoreType.DMA
    hidden_px = (plan.wr - 2) * plan.width
    feat_sends = 6 if rows == 4 else rows - 1
    scratch = [
        pltpu.VMEM((plan.pixels, depth), BF16),
        pltpu.VMEM((taps, 4 * own, depth), BF16),
        pltpu.VMEM((taps, depth, 4 * own), BF16),
        pltpu.VMEM((plan.fr * plan.fc, low_level.shape[2]), BF16),
        pltpu.VMEM(proj_weight.shape, BF16),
        pltpu.VMEM(conv1_weight.shape, BF16),
        pltpu.VMEM(conv2_weight.shape, BF16),
        pltpu.VMEM(up_own.shape[1:], BF16),
        pltpu.VMEM(up_side.shape[1:], BF16),
        pltpu.VMEM(plan.low_window().shape, BF16),
        pltpu.VMEM((3, plan.pixels, 4 * own), F32),
        pltpu.VMEM((3, 2, plan.half, 2 * own), BF16),
        pltpu.VMEM((3, 2, plan.half, 2 * own), BF16),
        pltpu.VMEM((cols, 8, own), F32),
        pltpu.VMEM((rows, 16, own), BF16),
        pltpu.VMEM((2, rows, plan.span, 2 * own), BF16),
        pltpu.VMEM((2, rows, plan.span, 2 * own), BF16),
        pltpu.VMEM((rows, 4 * own, out_width), BF16),
        pltpu.VMEM((2 * plan.cstrip, out_width), BF16),
        pltpu.VMEM((2, plan.cstrip, out_width), BF16),
        pltpu.VMEM((plan.low + 2 * plan.lstrip, red), BF16),
        pltpu.VMEM((2 * plan.lstrip, red), BF16),
        pltpu.VMEM((plan.window, red), BF16),
        pltpu.VMEM((2, hidden_px + 8, wide), F32),
        pltpu.VMEM((hidden_px, wide), F32),
        pltpu.VMEM((plan.window, out_width), BF16),
        pltpu.VMEM((hidden_px, wide), BF16),
        dma((8 + 4 * taps,)),
        dma((feat_sends,)), dma((feat_sends,)),
        dma((3, 2)), dma((3, 2)),
        dma((cols - 1,)), dma((cols - 1,)),
        dma((rows - 1,)), dma((rows - 1,)),
        dma((2, rows - 1)), dma((2, rows - 1)),
        dma((2,)), dma((2,)), dma((2,)), dma((2,)), dma((2,)), dma((2,)),
    ]
    return pl.pallas_call(
        functools.partial(kernel, plan),
        out_shape=jax.ShapeDtypeStruct((plan.fr, plan.fc, wide), BF16),
        in_specs=[
            any_spec, any_spec, any_spec, any_spec, any_spec, vmem, any_spec, vmem,
            vmem, vmem, any_spec, vmem, any_spec, vmem,
            any_spec, any_spec, vmem, vmem, vmem, any_spec,
        ],
        out_specs=vmem,
        scratch_shapes=scratch,
        compiler_params=pltpu.CompilerParams(
            collective_id=0, has_side_effects=True, vmem_limit_bytes=60 * 1024 * 1024
        ),
    )(
        jnp.transpose(features, (1, 0, 2)).reshape(plan.tile, depth),
        low_level.reshape(plan.fr * plan.fc, low_level.shape[2]),
        point_weight.T, jnp.swapaxes(atrous_weight, 3, 4), pool_weight.T, aspp_bias, proj_weight,
        proj_bias[None], low_weight.T, low_bias[None], conv1_weight, conv1_bias[None], conv2_weight, conv2_bias[None],
        jnp.asarray(up_own, BF16), jnp.asarray(up_side, BF16),
        jnp.asarray(plan.row_strips(), BF16), jnp.asarray(plan.coarse_strips(), BF16), jnp.asarray(plan.low_strips(), BF16),
        jnp.asarray(plan.low_window(), BF16),
    )


def solution(mesh):
    placed = (
        P(("dp", "row"), "col", None),
        P(("dp", "row"), "col", None),
        P(None, "row"),
        P(None, None, None, None, "row"),
        P(None, "row"),
        P(None, "row"),
        P(),
        P(),
        P(),
        P(),
        P(),
        P(),
        P(),
        P(),
    )

    def local(features, *others):
        plan = Plan(mesh.shape["row"], mesh.shape["col"], features.shape[0], features.shape[1])
        return on_device(plan, features, *others)

    return jax.shard_map(
        local,
        mesh=mesh,
        in_specs=placed,
        out_specs=P(("dp", "row"), "col", None),
        check_vma=False,
    )
```
